32 devices in a mesh: groups: 2 (over x), expert: 16 (over z, y, core).
Axes of the slice: x: 2, y: 2, z: 4, core: 2. Of those that a mesh axis runs over, the one named last changes fastest.
Arguments:
- tokens: bfloat16 [4096, 3584], P(('groups', 'expert')), parts along dimension 0, may hold values from -6 to 6
- expert_gate_up: bfloat16 [28672, 2048], P('expert'), may hold values from -0.09375 to 0.09375
- expert_down: bfloat16 [1024, 28672], P(None, 'expert'), may hold values from -0.1875 to 0.1875
- shared_gate_up: bfloat16 [3584, 2048], P('expert'), may hold values from -0.09375 to 0.09375
- shared_down: bfloat16 [1024, 3584], P(None, 'expert'), may hold values from -0.1875 to 0.1875
- host_expert: int32 [8], replicated, may hold values from 0 to 7, each once
- pair_picks: int32 [4096, 2], P(('groups', 'expert')), parts along dimension 0, may hold values from 0 to 7, all different within a row; in each aligned block of 128 rows (0 to 127, 128 to 255, ...) at most 56 rows name the same one
- affinity: float32 [4096, 8], P(('groups', 'expert')), parts along dimension 0, may hold values from 0.02 to 1
Outputs:
- mixed_rows: bfloat16 [4096, 3584], P(('groups', 'expert')), parts along dimension 0
The draws below stay inside these ranges and needn't reach their ends.
There are 2 independent parts, one for each index of `groups`. The reference program is written for one: setup_inputs(seed, part) draws one part's arguments, and reference() takes and returns one part's arrays. A program takes and returns all parts, laid end to end along the dimension named above; an argument that names none is the same for every part. Nothing has to cross between parts.
Inputs may be any that keep to these rules, and one draw needn't show every extreme that they name: host_expert names every expert id once. `pair_picks`: the 2 pairs of a token differ. Among the rows of one device no pair is named more than 56 times, a bound that some block reaches.
All inputs are finite; a program needn't handle non-finite values.
Results may differ from the reference program's by a relative error of at most 0.015.
Values may be sent and summed in bfloat16 or wider, within the bound.
No kernel may reach another device: no remote copies, remote signals or barrier semaphores. Data moves between devices by JAX's collectives and lax.ppermute only.
A program may use at most 128 MiB of HBM per device.

```python
import math
import jax
import jax.numpy as jnp
import numpy as np
from jax import lax

D = 3584
FF = 1024
TOP = 2
TOK_DEV = 128
EXPERTS = 8
CAP = 56
TOKENS = 2048
N_EXPERT = 16


def shard_levels(key, extent, shards, low, high):
    def one(dim, parts):
        steps = jax.random.uniform(jax.random.fold_in(jax.random.fold_in(key, 6), dim), (parts,), jnp.float32, low / len(shards), high / len(shards))
        return jnp.repeat(jnp.exp(steps), extent[dim] // parts).reshape((-1,) + (1,) * (len(extent) - dim - 1))

    level = one(*shards[0])
    for cut in shards[1:]:
        level = level * one(*cut)
    return level


def assign_block(stream_key, own, number, rows, count, top, limit, lean):
    ranking = jax.random.permutation(stream_key, count)
    heavy_load, ordinary = portions_of(count, rows * top, limit, lean, True), portions_of(count, rows * top, limit, lean, False)
    places = jnp.arange(count)

    def named(tallies, offset_by):
        used = int((tallies > 0).sum())
        fixed = max(1, used // 4)
        moved = fixed + (places - fixed + offset_by * (used - fixed)) % max(1, count - fixed)
        return jnp.zeros((count,), jnp.int32).at[ranking[jnp.where(places < fixed, places, moved)]].set(jnp.asarray(tallies, jnp.int32))

    tallies = jnp.where(number % 4 == 0, named(heavy_load, number // 4), named(ordinary, number - number // 4 - 1))
    mixed = jax.random.permutation(jax.random.fold_in(own, 3), count)
    source_of, sink = mixed[0:count // 2 * 2:2], mixed[1:count // 2 * 2:2]
    margin = jnp.minimum(tallies[source_of] - 1, limit - tallies[sink]) // 2
    margin = jnp.where((source_of == ranking[0]) | (sink == ranking[0]) | (tallies[sink] == 0), 0, jnp.maximum(margin, 0))
    moved = jax.random.randint(jax.random.fold_in(own, 4), (count // 2,), 0, 1 << 20) % (margin + 1)
    tallies = tallies.at[source_of].add(-moved).at[sink].add(moved)
    items = jnp.searchsorted(jnp.cumsum(tallies), jnp.arange(rows * top), side="right").astype(jnp.int32)
    listing = items.reshape(top, rows).T
    listing = listing[jax.random.permutation(jax.random.fold_in(own, 1), rows)]
    offset_by = jax.random.randint(jax.random.fold_in(own, 2), (rows, 1), 0, top)
    return jnp.take_along_axis(listing, (jnp.arange(top)[None, :] + offset_by) % top, axis=1)


def portions_of(number_of, total, bound, skew, full):
    loads = [(1 << 20) // math.isqrt(grade ** skew) + 1 for grade in range(1, number_of + 1)]
    largest = bound if full else min(bound, max(-(-total // number_of), total * loads[0] // sum(loads)))
    least = 1 if total - largest >= number_of - 1 else 0
    counts, rest = [largest] + [least] * (number_of - 1), total - largest - least * (number_of - 1)
    while rest > 0:
        candidates = [i for i in range(1, number_of) if counts[i] < largest] or [i for i in range(1, number_of) if counts[i] < bound]
        pool, budget = sum([loads[i] for i in candidates]), rest
        for i in candidates:
            more = min(bound - counts[i], max(1, budget * loads[i] // pool), rest)
            counts[i] = counts[i] + more
            rest = rest - more
    return np.array(counts)


def gaussian(rng, extent, spread, bound, cuts=(), kind=jnp.bfloat16):
    level = shard_levels(rng, extent, cuts, -0.22, 0.18) if cuts else 1.0
    entries = jax.random.normal(rng, extent, jnp.float32) * spread * level
    return jnp.minimum(jnp.maximum(entries, -bound), bound).astype(kind)


def setup_inputs(seed: int = 0, part: int = 0) -> dict:
    streams_of = jax.random.split(jax.random.key(seed), 9)
    part_splits = jax.random.split(jax.random.fold_in(streams_of[8], part), 9)
    tokens = gaussian(part_splits[0], (TOKENS, D), 1.0, 6.0, ((0, 16),))
    expert_gate_up = gaussian(streams_of[1], (EXPERTS * D, 2 * FF), D ** -0.5, 0.09375, ((0, 16),))
    expert_down = gaussian(streams_of[2], (FF, EXPERTS * D), FF ** -0.5, 0.1875, ((1, 16),))
    shared_gate_up = gaussian(streams_of[3], (D, 2 * FF), D ** -0.5, 0.09375, ((0, 16),))
    shared_down = gaussian(streams_of[4], (FF, D), FF ** -0.5, 0.1875, ((1, 16),))
    host_expert = jax.random.permutation(streams_of[5], EXPERTS).astype(jnp.int32)
    pair_picks_keys = jax.random.split(jax.random.fold_in(part_splits[6], 1), TOKENS // TOK_DEV)
    pair_picks_turns = jax.random.permutation(jax.random.fold_in(part_splits[6], 3), TOKENS // TOK_DEV)
    pair_picks = jax.vmap(lambda own, number: assign_block(jax.random.fold_in(part_splits[6], 2), own, number, TOK_DEV, EXPERTS, TOP, CAP, 2))(pair_picks_keys, pair_picks_turns).reshape((TOKENS, TOP))
    affinity = jnp.clip(jnp.exp(math.log(1.0) - 3.912023 * jax.random.uniform(part_splits[7], (TOKENS, EXPERTS), jnp.float32) ** shard_levels(part_splits[7], (TOKENS, EXPERTS), ((0, 16),), -0.2, 0.2)), 0.02, 1.0)
    return dict(tokens=tokens, expert_gate_up=expert_gate_up, expert_down=expert_down, shared_gate_up=shared_gate_up, shared_down=shared_down, host_expert=host_expert, pair_picks=pair_picks, affinity=affinity)


route_scale = 2.5


def swiglu(rows_in, gate_up, down):
    summed = jnp.dot(rows_in, gate_up, preferred_element_type=jnp.float32)
    hidden = (jax.nn.silu(summed[:, :FF]) * summed[:, FF:]).astype(jnp.bfloat16)
    return jnp.dot(hidden, down, preferred_element_type=jnp.float32).astype(jnp.bfloat16)


def reference(tokens, expert_gate_up, expert_down, shared_gate_up, shared_down, host_expert, pair_picks, affinity):
    half_width = D // 2
    gate_up_all = expert_gate_up.reshape(2, EXPERTS, half_width, 2 * FF).transpose(1, 0, 2, 3).reshape(EXPERTS, D, 2 * FF)
    down_all = expert_down.reshape(FF, 2, EXPERTS, half_width).transpose(2, 0, 1, 3).reshape(EXPERTS, FF, D)
    shared_rows = swiglu(tokens, shared_gate_up, shared_down)
    flat_picks = pair_picks.reshape(-1).astype(jnp.int32)
    pick_hits = (flat_picks[:, None] == jnp.arange(EXPERTS, dtype=jnp.int32)[None, :]).astype(jnp.int32)
    pick_ranks = jnp.sum(pick_hits * (jnp.cumsum(pick_hits, 0) - 1), 1).astype(jnp.int32)
    slot_count = N_EXPERT * CAP
    token_ids = (jnp.arange(TOKENS * TOP, dtype=jnp.int32) // TOP).astype(jnp.int32)
    slot_table = jnp.zeros((EXPERTS, slot_count), jnp.int32).at[flat_picks, pick_ranks].set(token_ids)

    def one_expert(pieces):
        table_row, gate_up, down = pieces
        return swiglu(tokens[table_row], gate_up, down)

    outputs = lax.map(one_expert, (slot_table, gate_up_all, down_all))
    picked = outputs[flat_picks, pick_ranks].astype(jnp.float32).reshape(TOKENS, TOP, D)
    expert_ids = host_expert[flat_picks].reshape(TOKENS, TOP).astype(jnp.int32)
    scores = jnp.take_along_axis(affinity, expert_ids, 1)
    gate_weights = route_scale * scores / jnp.sum(scores, 1, keepdims=True)
    mixed_rows = jnp.sum(picked * gate_weights[:, :, None], 1) + shared_rows.astype(jnp.float32)
    return mixed_rows.astype(jnp.bfloat16)
```

```python
import functools

import jax
import jax.numpy as jnp
from jax import lax
from jax.experimental import pallas as pl
from jax.experimental.pallas import tpu as pltpu
from jax.sharding import PartitionSpec as P

route_scale = 2.5
meta_lanes = 128
vmem_bytes = 48 * 1024 * 1024
f32 = jnp.float32
bf16 = jnp.bfloat16


def hop(block, mask, axis="expert"):
    count = lax.axis_size(axis)
    return lax.ppermute(block, axis, [(d, d ^ mask) for d in range(count)])


def low_bit(mask):
    return mask & -mask


def ordered(is_upper, own_part, other_part, axis_dim):
    return jnp.where(
        is_upper,
        jnp.concatenate([other_part, own_part], axis_dim),
        jnp.concatenate([own_part, other_part], axis_dim),
    )


def silu(v):
    return v / (1.0 + jnp.exp(-v))


def slots_of(meta, pair, lanes):
    m = meta.astype(f32)
    rows = m.shape[0]
    first = m[:, 0:1] == pair
    second = m[:, 1:2] == pair
    gate = jnp.where(first, m[:, 2:3] + m[:, 3:4], 0.0) + jnp.where(
        second, m[:, 4:5] + m[:, 5:6], 0.0
    )
    hit = jnp.where(first, 1.0, 0.0) + jnp.where(second, 1.0, 0.0)
    before = lax.broadcasted_iota(jnp.int32, (rows, rows), 1) < lax.broadcasted_iota(
        jnp.int32, (rows, rows), 0
    )
    wide_hit = jnp.broadcast_to(hit, (rows, lanes))
    rank = jnp.dot(
        jnp.where(before, 1.0, 0.0).astype(bf16), wide_hit.astype(bf16), preferred_element_type=f32
    )
    slot = lax.broadcasted_iota(jnp.int32, (rows, lanes), 1).astype(f32)
    one_hot = jnp.where(rank == slot, wide_hit, 0.0).astype(bf16)
    return one_hot, gate


def pick_rows(pair_ref, tok_ref, rows_ref):
    width = rows_ref.shape[1]
    pair = pair_ref[0].astype(f32)
    one_hot, _ = slots_of(tok_ref[:, width:], pair, rows_ref.shape[0])
    rows_ref[...] = lax.dot_general(
        one_hot, tok_ref[:, :width], (((0,), (0,)), ((), ())), preferred_element_type=f32
    ).astype(bf16)


def partial_kernel(pair_ref, tok_ref, w_ref, out_ref, rows_ref):
    @pl.when(pl.program_id(0) == 0)
    def _():
        pick_rows(pair_ref, tok_ref, rows_ref)

    out_ref[...] = jnp.dot(rows_ref[...], w_ref[...], preferred_element_type=f32)[
        : out_ref.shape[0]
    ].astype(bf16)


def hidden_kernel(pair_ref, tok_ref, wg_ref, wu_ref, rg_ref, ru_ref, out_ref, rows_ref):
    @pl.when(pl.program_id(0) == 0)
    def _():
        pick_rows(pair_ref, tok_ref, rows_ref)

    cap = out_ref.shape[0]
    rows = rows_ref[...]
    gate = jnp.dot(rows, wg_ref[...], preferred_element_type=f32)[:cap] + rg_ref[...].astype(f32)
    up = jnp.dot(rows, wu_ref[...], preferred_element_type=f32)[:cap] + ru_ref[...].astype(f32)
    out_ref[...] = (silu(gate) * up).astype(bf16)


def down_kernel(pair_ref, meta_ref, hid_ref, w_ref, out_ref, hit_ref, gate_ref, rows_ref):
    @pl.when(pl.program_id(0) == 0)
    def _():
        one_hot, gate = slots_of(meta_ref[...], pair_ref[0].astype(f32), hit_ref.shape[1])
        hit_ref[...] = one_hot
        gate_ref[...] = jnp.broadcast_to(gate, gate_ref.shape)
        rows_ref[...] = jnp.zeros_like(rows_ref)

    cap = hid_ref.shape[0]
    rows_ref[:cap, :] = jnp.dot(hid_ref[...], w_ref[...], preferred_element_type=f32).astype(bf16)
    picked = jnp.dot(hit_ref[...], rows_ref[...], preferred_element_type=f32)
    out_ref[...] = (picked * gate_ref[:, 0:1]).astype(bf16)


def params():
    return pltpu.CompilerParams(
        vmem_limit_bytes=vmem_bytes, dimension_semantics=("arbitrary",)
    )


def smem():
    return pl.BlockSpec(memory_space=pltpu.SMEM)


def whole(array):
    return pl.BlockSpec(array.shape, lambda j: (0, 0))


def cost(m, k, n):
    return pl.CostEstimate(flops=2 * m * k * n, bytes_accessed=2 * k * n, transcendentals=0)


def partial_sums(pair, tok, weights, cap, cap_lanes):
    width, columns = weights.shape
    steps = 4
    return pl.pallas_call(
        partial_kernel,
        grid=(steps,),
        in_specs=[
            smem(),
            whole(tok),
            pl.BlockSpec((width, columns // steps), lambda j: (0, j)),
        ],
        out_specs=pl.BlockSpec((cap, columns // steps), lambda j: (0, j)),
        out_shape=jax.ShapeDtypeStruct((cap, columns), bf16),
        scratch_shapes=[pltpu.VMEM((cap_lanes, width), bf16)],
        compiler_params=params(),
        cost_estimate=cost(cap_lanes, width, columns),
    )(pair, tok, weights)


def hidden_rows(pair, tok, weights, received, cap_lanes):
    width, columns = weights.shape
    units = columns // 2
    cap = received.shape[0]
    steps = 4
    block = units // steps
    return pl.pallas_call(
        hidden_kernel,
        grid=(steps,),
        in_specs=[
            smem(),
            whole(tok),
            pl.BlockSpec((width, block), lambda j: (0, j)),
            pl.BlockSpec((width, block), lambda j: (0, j + steps)),
            pl.BlockSpec((cap, block), lambda j: (0, j)),
            pl.BlockSpec((cap, block), lambda j: (0, j + steps)),
        ],
        out_specs=pl.BlockSpec((cap, block), lambda j: (0, j)),
        out_shape=jax.ShapeDtypeStruct((cap, units), bf16),
        scratch_shapes=[pltpu.VMEM((cap_lanes, width), bf16)],
        compiler_params=params(),
        cost_estimate=cost(cap_lanes, width, columns),
    )(pair, tok, weights, weights, received, received)


def weighted_rows(pair, tok, hidden, weights, cap_lanes):
    units, width = weights.shape
    cap = hidden.shape[0]
    count = tok.shape[0]
    steps = 2
    block = width // steps
    return pl.pallas_call(
        down_kernel,
        grid=(steps,),
        in_specs=[
            smem(),
            pl.BlockSpec((count, meta_lanes), lambda j: (0, width // meta_lanes)),
            whole(hidden),
            pl.BlockSpec((units, block), lambda j: (0, j)),
        ],
        out_specs=pl.BlockSpec((count, block), lambda j: (0, j)),
        out_shape=jax.ShapeDtypeStruct((count, width), bf16),
        scratch_shapes=[
            pltpu.VMEM((count, cap_lanes), bf16),
            pltpu.VMEM((count, meta_lanes), f32),
            pltpu.VMEM((cap_lanes, block), bf16),
        ],
        compiler_params=params(),
        cost_estimate=cost(cap_lanes, units, width),
    )(pair, tok, hidden, weights)


def shared_gate_kernel(parts, spots_ref, own_ref, other_ref, *refs):
    blocks, (mine_ref, theirs_ref, w_ref, sems) = refs[: len(parts)], refs[len(parts) :]
    copies = []
    for block, (row_spot, column_spot) in zip(blocks, parts):
        for i in range(block.shape[0]):
            rows, columns = block.shape[1:]
            row = pl.multiple_of(spots_ref[row_spot + i] * rows, rows)
            column = pl.multiple_of(spots_ref[column_spot] * columns, columns)
            copies.append(
                pltpu.make_async_copy(
                    block.at[i],
                    w_ref.at[pl.ds(row, rows), pl.ds(column, columns)],
                    sems.at[len(copies)],
                )
            )
    for copy in copies:
        copy.start()
    for copy in copies:
        copy.wait()
    width, columns = w_ref.shape
    step = 512

    @pl.loop(0, columns // step)
    def _(j):
        at = pl.ds(pl.multiple_of(j * step, step), step)
        w = w_ref[:, at]
        mine_ref[:, at] = jnp.dot(own_ref[:, :width], w, preferred_element_type=f32).astype(bf16)
        theirs_ref[:, at] = jnp.dot(other_ref[:, :width], w, preferred_element_type=f32)


def shared_partial(spots, own, other, blocks, parts, width, columns):
    rows = own.shape[0]
    vmem = pl.BlockSpec(memory_space=pltpu.VMEM)
    return pl.pallas_call(
        functools.partial(shared_gate_kernel, parts),
        in_specs=[smem(), vmem, vmem] + [pl.BlockSpec(memory_space=pl.ANY)] * len(blocks),
        out_specs=[vmem, vmem],
        out_shape=[
            jax.ShapeDtypeStruct((rows, columns), bf16),
            jax.ShapeDtypeStruct((rows, columns), f32),
        ],
        scratch_shapes=[
            pltpu.VMEM((width, columns), bf16),
            pltpu.SemaphoreType.DMA((sum(b.shape[0] for b in blocks),)),
        ],
        compiler_params=pltpu.CompilerParams(vmem_limit_bytes=vmem_bytes),
        cost_estimate=cost(2 * rows, width, columns),
    )(spots, own, other, *blocks)


def shared_down_kernel(parts, spots_ref, mine_ref, theirs_ref, *refs):
    blocks, (out_ref, d_ref, sems) = refs[: len(parts)], refs[len(parts) :]
    copies = []
    for block, (spot, row_spot) in zip(blocks, parts):
        for i in range(block.shape[0]):
            rows = block.shape[1]
            row = pl.multiple_of(spots_ref[row_spot] * rows, rows)
            copies.append(
                pltpu.make_async_copy(
                    block.at[i],
                    d_ref.at[spots_ref[spot + i], pl.ds(row, rows), :],
                    sems.at[len(copies)],
                )
            )
    for copy in copies:
        copy.start()
    for copy in copies:
        copy.wait()
    count = mine_ref.shape[0]

    @pl.loop(0, d_ref.shape[0])
    def _(i):
        d = d_ref[i]
        out_ref[i, :count, :] = jnp.dot(mine_ref[...], d, preferred_element_type=f32).astype(bf16)
        out_ref[i, count:, :] = jnp.dot(theirs_ref[...], d, preferred_element_type=f32).astype(bf16)


def shared_rows(spots, mine, theirs, blocks, parts, shards):
    rows, units = mine.shape
    columns = blocks[0].shape[2]
    vmem = pl.BlockSpec(memory_space=pltpu.VMEM)
    return pl.pallas_call(
        functools.partial(shared_down_kernel, parts),
        in_specs=[smem(), vmem, vmem] + [pl.BlockSpec(memory_space=pl.ANY)] * len(blocks),
        out_specs=vmem,
        out_shape=jax.ShapeDtypeStruct((shards, 2 * rows, columns), bf16),
        scratch_shapes=[
            pltpu.VMEM((shards, units, columns), bf16),
            pltpu.SemaphoreType.DMA((sum(b.shape[0] for b in blocks),)),
        ],
        compiler_params=pltpu.CompilerParams(vmem_limit_bytes=vmem_bytes),
        cost_estimate=cost(2 * rows, units, shards * columns),
    )(spots, mine, theirs, *blocks)


def gather_blocks(block, hops, groups):
    stack = block[None]
    for bit in hops:
        stack = jnp.concatenate([stack, hop(stack, bit)], 0)
    stacks = [stack]
    bit = 1
    while bit < groups:
        stacks = stacks + [hop(s, bit, "groups") for s in stacks]
        bit *= 2
    return stacks + [hop(s, 1) for s in stacks]


def in_order(blocks, stack_masks, place, group_index):
    chips = len(stack_masks)
    groups = len(blocks) // 2
    stacked = jnp.stack(blocks).reshape((2, groups, chips) + blocks[0].shape[1:])
    spot = [0] * chips
    for i, mask in enumerate(stack_masks):
        spot[mask // 2] = i
    mask = jnp.arange(2 * chips, dtype=jnp.int32) ^ place
    by_core = stacked.transpose(0, 2, 1, 3, 4).reshape((2 * chips, groups) + blocks[0].shape[1:])
    by_shard = by_core[(mask & 1) * chips + jnp.array(spot, jnp.int32)[mask // 2]]
    return by_shard[:, group_index ^ jnp.arange(groups, dtype=jnp.int32)]


def local(
    tokens,
    expert_gate_up,
    expert_down,
    shared_gate_up,
    shared_down,
    host_expert,
    pair_picks,
    affinity,
):
    devices = lax.axis_size("expert")
    groups = lax.axis_size("groups")
    half = devices // 2
    dev_index = lax.axis_index("expert")
    group_index = lax.axis_index("groups")
    place = dev_index % half
    is_upper = dev_index >= half
    pair = jnp.reshape(place, (1,)).astype(jnp.int32)
    tok_rows, full_width = tokens.shape
    width = full_width // 2
    units = expert_down.shape[0]
    pick_count = pair_picks.shape[1]
    capacity = 7 * tok_rows * pick_count // (4 * half)
    cap = -(-2 * capacity // 16) * 16
    cap_lanes = -(-cap // 128) * 128
    chips = list(range(0, half, 2))
    hops = []
    bit = half // 2
    while bit > 1:
        hops.append(bit)
        bit //= 2

    pair_iota = jnp.arange(half, dtype=jnp.int32)
    expert_ids = jnp.sum(
        jnp.where(pair_picks[:, :, None] == pair_iota, host_expert[None, None, :], 0), 2
    )
    scores = jnp.sum(
        jnp.where(expert_ids[:, :, None] == pair_iota, affinity[:, None, :], 0.0), 2
    )
    gates = route_scale * scores / jnp.sum(scores, 1, keepdims=True)
    gates_high = lax.reduce_precision(gates, 8, 7)
    gates_low = gates - gates_high
    meta = jnp.concatenate(
        [
            pair_picks.astype(f32),
            jnp.stack([gates_high, gates_low], 2).reshape(tok_rows, 2 * pick_count),
            jnp.zeros((tok_rows, meta_lanes - 3 * pick_count), f32),
        ],
        1,
    ).astype(bf16)
    low, high = tokens[:, :width], tokens[:, width:]
    mine = jnp.concatenate([jnp.where(is_upper, high, low), meta], 1)
    theirs = jnp.concatenate([jnp.where(is_upper, low, high), meta], 1)

    cross = hop(theirs, half)

    def spread(block):
        got = {0: block}
        for mask in sorted(chips[1:], key=lambda m: (bin(m).count("1"), -m)):
            got[mask] = hop(got[mask ^ low_bit(mask)], low_bit(mask))
        return {m: jnp.concatenate([b, hop(b, 1)], 0) for m, b in got.items()}

    order = sorted(chips[1:], key=lambda m: (bin(m).count("1"), -m)) + [0]
    home = spread(mine)
    sums_out = {m: partial_sums(pair, home[m], expert_gate_up, cap, cap_lanes) for m in order}
    sums_in = {m: hop(sums_out[m], half) for m in order}
    away = spread(cross)
    away_hidden = {
        m: hidden_rows(pair, away[m], expert_gate_up, sums_in[m], cap_lanes) for m in order
    }
    home_hidden = {m: hop(away_hidden[m], half) for m in order}

    gate_columns = shared_gate_up.shape[1] // groups
    down_rows = units // groups
    gate_blocks = gather_blocks(
        lax.dynamic_slice_in_dim(shared_gate_up, group_index * gate_columns, gate_columns, 1),
        hops,
        groups,
    )
    down_blocks = gather_blocks(
        lax.dynamic_slice_in_dim(shared_down, group_index * down_rows, down_rows, 0), hops, groups
    )
    stack_masks = [0]
    for bit in hops:
        stack_masks = stack_masks + [m | bit for m in stack_masks]
    chip_count = len(chips)
    masks = jnp.array(stack_masks, jnp.int32)
    spots = jnp.concatenate(
        [place ^ masks, place ^ 1 ^ masks, group_index ^ jnp.arange(groups, dtype=jnp.int32)]
    ).astype(jnp.int32)
    parts = [(core * chip_count, 2 * chip_count + g) for core in (0, 1) for g in range(groups)]
    by_kernel = shared_gate_up.shape[0] % 16 == 0
    if by_kernel:
        own_sums, other_sums = shared_partial(
            spots, mine, cross, gate_blocks, parts, width, shared_gate_up.shape[1]
        )
    else:
        gate_rows = in_order(gate_blocks, stack_masks, place, group_index)
        gate_rows = gate_rows.transpose(0, 2, 1, 3).reshape(width, 2 * units)
        own_sums = jnp.dot(mine[:, :width], gate_rows, preferred_element_type=f32).astype(bf16)
        other_sums = jnp.dot(cross[:, :width], gate_rows, preferred_element_type=f32)
    total = other_sums + hop(own_sums, half).astype(f32)
    other_hidden = (silu(total[:, :units]) * total[:, units:]).astype(bf16)
    own_hidden = hop(other_hidden, half)
    if by_kernel:
        shared_out = shared_rows(spots, own_hidden, other_hidden, down_blocks, parts, half)
        shared_out = shared_out.transpose(1, 0, 2).reshape(2 * tok_rows, width).astype(f32)
    else:
        down_columns = in_order(down_blocks, stack_masks, place, group_index)
        down_columns = down_columns.transpose(1, 2, 0, 3).reshape(units, width)
        both = jnp.concatenate([own_hidden, other_hidden], 0)
        shared_out = jnp.dot(both, down_columns, preferred_element_type=f32)
        shared_out = shared_out.astype(bf16).astype(f32)

    def collect(tok, hidden):
        total = {}
        for m in order:
            rows = weighted_rows(pair, tok[m], hidden[m], expert_down, cap_lanes)
            total[m] = rows[:tok_rows].astype(f32) + hop(rows[tok_rows:], 1).astype(f32)
        for bit in hops[::-1]:
            for m in [m for m in order if m in total and low_bit(m) == bit]:
                sent = hop(total.pop(m).astype(bf16), bit)
                total[m ^ bit] = total[m ^ bit] + sent.astype(f32)
        return total[0]

    away_rows = (collect(away, away_hidden) + shared_out[tok_rows:]).astype(bf16)
    far_half = hop(away_rows, half)
    near_half = (collect(home, home_hidden) + shared_out[:tok_rows]).astype(bf16)
    return ordered(is_upper, near_half, far_half, 1)


def solution(mesh):
    in_specs = (
        P(("groups", "expert"), None),
        P("expert", None),
        P(None, "expert"),
        P("expert", None),
        P(None, "expert"),
        P(),
        P(("groups", "expert"), None),
        P(("groups", "expert"), None),
    )
    out_specs = P(("groups", "expert"), None)
    return jax.shard_map(local, mesh=mesh, in_specs=in_specs, out_specs=out_specs, check_vma=False)
```

```python
import functools

import jax
import jax.numpy as jnp
from jax import lax
from jax.experimental import pallas as pl
from jax.experimental.pallas import tpu as pltpu
from jax.sharding import PartitionSpec as P

route_scale = 2.5
meta_lanes = 128
vmem_bytes = 48 * 1024 * 1024
f32 = jnp.float32
bf16 = jnp.bfloat16


def hop(block, mask, axis="expert"):
    count = lax.axis_size(axis)
    return lax.ppermute(block, axis, [(d, d ^ mask) for d in range(count)])


def settle(*values):
    return lax.optimization_barrier(values)


def ordered(is_upper, own_part, other_part, axis_dim):
    return jnp.where(
        is_upper,
        jnp.concatenate([other_part, own_part], axis_dim),
        jnp.concatenate([own_part, other_part], axis_dim),
    )


def silu(v):
    return v / (1.0 + jnp.exp(-v))


def slots_of(meta, pair, lanes):
    m = meta.astype(f32)
    rows = m.shape[0]
    first = m[:, 0:1] == pair
    second = m[:, 1:2] == pair
    gate = jnp.where(first, m[:, 2:3] + m[:, 3:4], 0.0) + jnp.where(
        second, m[:, 4:5] + m[:, 5:6], 0.0
    )
    hit = jnp.where(first, 1.0, 0.0) + jnp.where(second, 1.0, 0.0)
    before = lax.broadcasted_iota(jnp.int32, (rows, rows), 1) < lax.broadcasted_iota(
        jnp.int32, (rows, rows), 0
    )
    wide_hit = jnp.broadcast_to(hit, (rows, lanes))
    rank = jnp.dot(
        jnp.where(before, 1.0, 0.0).astype(bf16), wide_hit.astype(bf16), preferred_element_type=f32
    )
    slot = lax.broadcasted_iota(jnp.int32, (rows, lanes), 1).astype(f32)
    one_hot = jnp.where(rank == slot, wide_hit, 0.0).astype(bf16)
    return one_hot, gate


def pick_rows(pair_ref, first_ref, second_ref, rows_ref, cap):
    width = rows_ref.shape[1]
    count = first_ref.shape[1]
    pair = pair_ref[0].astype(f32)
    lanes = -(-cap // 128) * 128
    dims = (((0,), (0,)), ((), ()))
    for q in range(first_ref.shape[0]):
        meta = jnp.concatenate([first_ref[q, :, width:], second_ref[q, :, width:]], 0)
        one_hot, _ = slots_of(meta, pair, lanes)
        rows = lax.dot_general(
            one_hot[:count], first_ref[q, :, :width], dims, preferred_element_type=f32
        ) + lax.dot_general(
            one_hot[count:], second_ref[q, :, :width], dims, preferred_element_type=f32
        )
        rows_ref[q * cap : (q + 1) * cap, :] = rows[:cap].astype(bf16)


def partial_kernel(cap, pair_ref, first_ref, second_ref, w_ref, out_ref, rows_ref):
    @pl.when(pl.program_id(0) == 0)
    def _():
        pick_rows(pair_ref, first_ref, second_ref, rows_ref, cap)

    out_ref[...] = jnp.dot(
        rows_ref[...], w_ref[...], preferred_element_type=f32
    ).astype(bf16)


def hidden_kernel(
    cap, pair_ref, first_ref, second_ref, wg_ref, wu_ref, rg_ref, ru_ref, out_ref, rows_ref
):
    @pl.when(pl.program_id(0) == 0)
    def _():
        pick_rows(pair_ref, first_ref, second_ref, rows_ref, cap)

    rows = rows_ref[...]
    gate = jnp.dot(rows, wg_ref[...], preferred_element_type=f32) + rg_ref[...].astype(f32)
    up = jnp.dot(rows, wu_ref[...], preferred_element_type=f32) + ru_ref[...].astype(f32)
    out_ref[...] = (silu(gate) * up).astype(bf16)


def down_kernel(
    cap,
    pair_ref,
    first_ref,
    second_ref,
    hid_ref,
    w_ref,
    near_ref,
    far_ref,
    hit_ref,
    gate_ref,
    rows_ref,
):
    chips, count, _ = near_ref.shape

    @pl.when(pl.program_id(0) == 0)
    def _():
        for q in range(chips):
            meta = jnp.concatenate([first_ref[q], second_ref[q]], 0)
            one_hot, gate = slots_of(meta, pair_ref[0].astype(f32), hit_ref.shape[2])
            hit_ref[q] = one_hot
            gate_ref[q] = jnp.broadcast_to(gate, gate_ref.shape[1:])
        rows_ref[...] = jnp.zeros_like(rows_ref)

    rows = jnp.dot(hid_ref[...], w_ref[...], preferred_element_type=f32).astype(bf16)
    for q in range(chips):
        rows_ref[q, :cap, :] = rows[q * cap : (q + 1) * cap]
        picked = jnp.dot(hit_ref[q], rows_ref[q], preferred_element_type=f32)
        gated = (picked * gate_ref[q, :, 0:1]).astype(bf16)
        near_ref[q] = gated[:count]
        far_ref[q] = gated[count:]


def params():
    return pltpu.CompilerParams(
        vmem_limit_bytes=vmem_bytes, dimension_semantics=("arbitrary",)
    )


def smem():
    return pl.BlockSpec(memory_space=pltpu.SMEM)


def whole(array):
    return pl.BlockSpec(array.shape, lambda j: (0,) * len(array.shape))


def cost(m, k, n):
    return pl.CostEstimate(flops=0, bytes_accessed=0, transcendentals=0)


def partial_sums(pair, tok, weights, cap):
    width, columns = weights.shape
    rows = tok[0].shape[0] * cap
    steps = 4
    return pl.pallas_call(
        functools.partial(partial_kernel, cap),
        grid=(steps,),
        in_specs=[
            smem(),
            whole(tok[0]),
            whole(tok[1]),
            pl.BlockSpec((width, columns // steps), lambda j: (0, j)),
        ],
        out_specs=pl.BlockSpec((rows, columns // steps), lambda j: (0, j)),
        out_shape=jax.ShapeDtypeStruct((rows, columns), bf16),
        scratch_shapes=[pltpu.VMEM((rows, width), bf16)],
        compiler_params=params(),
        cost_estimate=cost(rows, width, columns),
    )(pair, *tok, weights)


def hidden_rows(pair, tok, weights, received, cap):
    width, columns = weights.shape
    units = columns // 2
    rows = received.shape[0]
    steps = 4
    block = units // steps
    return pl.pallas_call(
        functools.partial(hidden_kernel, cap),
        grid=(steps,),
        in_specs=[
            smem(),
            whole(tok[0]),
            whole(tok[1]),
            pl.BlockSpec((width, block), lambda j: (0, j)),
            pl.BlockSpec((width, block), lambda j: (0, j + steps)),
            pl.BlockSpec((rows, block), lambda j: (0, j)),
            pl.BlockSpec((rows, block), lambda j: (0, j + steps)),
        ],
        out_specs=pl.BlockSpec((rows, block), lambda j: (0, j)),
        out_shape=jax.ShapeDtypeStruct((rows, units), bf16),
        scratch_shapes=[pltpu.VMEM((rows, width), bf16)],
        compiler_params=params(),
        cost_estimate=cost(rows, width, columns),
    )(pair, *tok, weights, weights, received, received)


def weighted_rows(pair, tok, hidden, weights, cap):
    units, width = weights.shape
    chips, count, _ = tok[0].shape
    lanes = -(-cap // 128) * 128
    steps = 2
    block = width // steps
    meta = pl.BlockSpec((chips, count, meta_lanes), lambda j: (0, 0, width // meta_lanes))
    return pl.pallas_call(
        functools.partial(down_kernel, cap),
        grid=(steps,),
        in_specs=[
            smem(),
            meta,
            meta,
            whole(hidden),
            pl.BlockSpec((units, block), lambda j: (0, j)),
        ],
        out_specs=[pl.BlockSpec((chips, count, block), lambda j: (0, 0, j))] * 2,
        out_shape=[jax.ShapeDtypeStruct((chips, count, width), bf16)] * 2,
        scratch_shapes=[
            pltpu.VMEM((chips, 2 * count, lanes), bf16),
            pltpu.VMEM((chips, 2 * count, 128), f32),
            pltpu.VMEM((chips, lanes, block), bf16),
        ],
        compiler_params=params(),
        cost_estimate=cost(chips * cap, units, width),
    )(pair, *tok, hidden, weights)


def assemble(masks, first_column, spots_ref, stack_refs, out_ref, sems):
    count, rows, _ = stack_refs[0].shape
    columns = out_ref.shape[1] // len({q for _, _, q in masks})
    copies = []
    for core, stack_ref in enumerate(stack_refs):
        for i, (upper, _, q) in enumerate(masks):
            shard = spots_ref[core * count + i]
            row = pl.multiple_of(shard * 2 * rows + upper * rows, rows)
            column = pl.multiple_of(spots_ref[2 * count + q] * columns, columns)
            copies.append(
                pltpu.make_async_copy(
                    stack_ref.at[i, :, pl.ds(first_column, columns)],
                    out_ref.at[pl.ds(row, rows), pl.ds(column, columns)],
                    sems.at[len(copies)],
                )
            )
    for copy in copies:
        copy.start()
    for copy in copies:
        copy.wait()


def shared_gate_kernel(
    masks, spots_ref, own_ref, other_ref, a_ref, b_ref, mine_ref, theirs_ref, w_ref, sems
):
    assemble(masks, 0, spots_ref, (a_ref, b_ref), w_ref, sems)
    width, columns = w_ref.shape
    step = 512

    @pl.loop(0, columns // step)
    def _(j):
        at = pl.ds(pl.multiple_of(j * step, step), step)
        w = w_ref[:, at]
        mine_ref[:, at] = jnp.dot(own_ref[:, :width], w, preferred_element_type=f32).astype(bf16)
        theirs_ref[:, at] = jnp.dot(other_ref[:, :width], w, preferred_element_type=f32)


def shared_partial(spots, masks, own, other, stacks, width, columns):
    rows = own.shape[0]
    vmem = pl.BlockSpec(memory_space=pltpu.VMEM)
    hbm = pl.BlockSpec(memory_space=pl.ANY)
    return pl.pallas_call(
        functools.partial(shared_gate_kernel, masks),
        in_specs=[smem(), vmem, vmem, hbm, hbm],
        out_specs=[vmem, vmem],
        out_shape=[
            jax.ShapeDtypeStruct((rows, columns), bf16),
            jax.ShapeDtypeStruct((rows, columns), f32),
        ],
        scratch_shapes=[
            pltpu.VMEM((width, columns), bf16),
            pltpu.SemaphoreType.DMA((2 * len(masks),)),
        ],
        compiler_params=pltpu.CompilerParams(vmem_limit_bytes=vmem_bytes),
        cost_estimate=cost(2 * rows, width, columns),
    )(spots, own, other, *stacks)


def shared_down_kernel(
    masks, first_column, spots_ref, hid_ref, a_ref, b_ref, out_ref, d_ref, sems
):
    assemble(masks, first_column, spots_ref, (a_ref, b_ref), d_ref, sems)
    step = 256

    @pl.loop(0, d_ref.shape[0] // step)
    def _(j):
        at = pl.ds(pl.multiple_of(j * step, step), step)
        out_ref[:, at] = lax.dot_general(
            hid_ref[...], d_ref[at, :], (((1,), (1,)), ((), ())), preferred_element_type=f32
        ).astype(bf16)


def shared_rows(spots, masks, hidden, stacks, first_column, width):
    rows, units = hidden.shape
    vmem = pl.BlockSpec(memory_space=pltpu.VMEM)
    hbm = pl.BlockSpec(memory_space=pl.ANY)
    return pl.pallas_call(
        functools.partial(shared_down_kernel, masks, first_column),
        in_specs=[smem(), vmem, hbm, hbm],
        out_specs=vmem,
        out_shape=jax.ShapeDtypeStruct((rows, width), bf16),
        scratch_shapes=[
            pltpu.VMEM((width, units), bf16),
            pltpu.SemaphoreType.DMA((2 * len(masks),)),
        ],
        compiler_params=pltpu.CompilerParams(vmem_limit_bytes=vmem_bytes),
        cost_estimate=cost(rows, units, width),
    )(spots, hidden, *stacks)


def in_order(masks, place, group_index, stacks):
    groups = len({q for _, _, q in masks})
    shards = len(masks) // groups
    spot = {}
    for core in (0, 1):
        for i, (upper, m, q) in enumerate(masks):
            spot[m | core, upper, q] = core * len(masks) + i
    table = [[[spot[m, u, q] for q in range(groups)] for u in (0, 1)] for m in range(shards)]
    table = jnp.array(table, jnp.int32)
    table = table[jnp.arange(shards, dtype=jnp.int32) ^ place]
    table = table[:, :, jnp.arange(groups, dtype=jnp.int32) ^ group_index]
    parts = jnp.concatenate(stacks)[table]
    parts = parts.transpose(0, 1, 3, 2, 4)
    return parts.reshape(shards, -1, groups, parts.shape[-1])


def local(
    tokens,
    expert_gate_up,
    expert_down,
    shared_gate_up,
    shared_down,
    host_expert,
    pair_picks,
    affinity,
):
    devices = lax.axis_size("expert")
    groups = lax.axis_size("groups")
    half = devices // 2
    dev_index = lax.axis_index("expert")
    group_index = lax.axis_index("groups")
    is_upper = dev_index >= half
    pair = jnp.reshape(dev_index % half, (1,)).astype(jnp.int32)
    tok_rows, full_width = tokens.shape
    width = full_width // 2
    units = expert_down.shape[0]
    pick_count = pair_picks.shape[1]
    capacity = 7 * tok_rows * pick_count // (4 * half)
    cap = -(-2 * capacity // 16) * 16
    chips = list(range(2, half, 2))
    near_chips = sorted([m for m in chips if m & (m - 1) == 0], reverse=True)
    far_chips = [m for m in chips if m & (m - 1)]

    pair_iota = jnp.arange(half, dtype=jnp.int32)
    expert_ids = jnp.sum(
        jnp.where(pair_picks[:, :, None] == pair_iota, host_expert[None, None, :], 0), 2
    )
    scores = jnp.sum(
        jnp.where(expert_ids[:, :, None] == pair_iota, affinity[:, None, :], 0.0), 2
    )
    gates = route_scale * scores / jnp.sum(scores, 1, keepdims=True)
    gates_high = lax.reduce_precision(gates, 8, 7)
    gates_low = gates - gates_high
    meta = jnp.concatenate(
        [
            pair_picks.astype(f32),
            jnp.stack([gates_high, gates_low], 2).reshape(tok_rows, 2 * pick_count),
            jnp.zeros((tok_rows, meta_lanes - 3 * pick_count), f32),
        ],
        1,
    ).astype(bf16)
    low, high = tokens[:, :width], tokens[:, width:]
    mine = jnp.concatenate([jnp.where(is_upper, high, low), meta], 1)
    theirs = jnp.concatenate([jnp.where(is_upper, low, high), meta], 1)

    def sums_of(tok):
        return partial_sums(pair, tok, expert_gate_up, cap)

    def hidden_of(tok, sums):
        return hidden_rows(pair, tok, expert_gate_up, sums, cap)

    def rows_of(tok, hidden):
        return weighted_rows(pair, tok, hidden, expert_down, cap)

    def summed(rows, other):
        return (rows.astype(f32) + other.astype(f32)).astype(bf16)

    def hops_of(blocks, masks):
        return [hop(block, m) for m, block in zip(masks, blocks)]

    def finished(shared, rows, other, parts):
        total = shared.astype(f32) + rows[0].astype(f32) + other.astype(f32)
        for part in parts:
            total = total + part.astype(f32)
        return total.astype(bf16)

    low_bit = near_chips[-1]
    group_bits = [1 << i for i in range(groups.bit_length() - 1)]
    gate_columns = 2 * units // groups
    down_rows = units // groups
    shard_rows = shared_gate_up.shape[0]
    upper_row = shard_rows // 2

    def share_of_weights():
        gate = lax.dynamic_slice_in_dim(shared_gate_up, group_index * gate_columns, gate_columns, 1)
        down = lax.dynamic_slice_in_dim(shared_down, group_index * down_rows, down_rows, 0)
        return jnp.concatenate([gate, down.T], 1)[None]

    def doubled(stack, bits, axis="expert"):
        for bit in bits:
            stack = jnp.concatenate([stack, hop(stack, bit, axis)])
        return stack

    def masks_of(upper, steps):
        masks = [(0, 0)]
        for m, q in steps:
            masks = masks + [(a ^ m, b ^ q) for a, b in masks]
        return [(upper, a, b) for a, b in masks]

    far_steps = [(m, 0) for m in near_chips[:-1]]
    group_steps = [(0, q) for q in group_bits]
    low_steps = [(low_bit, 0)]
    masks = masks_of(0, far_steps + group_steps + low_steps) + masks_of(
        1, far_steps + low_steps + group_steps
    )
    place = dev_index % half
    chip_masks = jnp.array([m for _, m, _ in masks], jnp.int32)
    spots = jnp.concatenate(
        [place ^ chip_masks, place ^ 1 ^ chip_masks, group_index ^ jnp.arange(groups)]
    ).astype(jnp.int32)
    by_kernel = upper_row % 16 == 0

    def shared_sums(stacks):
        if by_kernel:
            return shared_partial(spots, masks, mine, cross, stacks, width, 2 * units)
        gate = in_order(masks, place, group_index, stacks)[..., :gate_columns]
        gate = gate.reshape(width, 2 * units)
        own = jnp.dot(mine[:, :width], gate, preferred_element_type=f32).astype(bf16)
        return own, jnp.dot(cross[:, :width], gate, preferred_element_type=f32)

    def shared_down_of(hidden, stacks):
        if by_kernel:
            return shared_rows(spots, masks, hidden, stacks, gate_columns, width)
        down = in_order(masks, place, group_index, stacks)[..., gate_columns:]
        down = down.reshape(width, units)
        return lax.dot_general(
            hidden, down, (((1,), (1,)), ((), ())), preferred_element_type=f32
        ).astype(bf16)

    cross = hop(theirs, half)
    near = [hop(mine, m) for m in near_chips]
    own_tok = mine[None], hop(mine, 1)[None]
    own_sums = sums_of(own_tok)
    weights = share_of_weights()
    cross, near, own_tok, own_sums, weights = settle(cross, near, own_tok, own_sums, weights)

    own_in = hop(own_sums, half)
    got = dict(zip(near_chips, near))
    away_near = [hop(cross, m) for m in near_chips[:-1]]
    near_tok = jnp.stack(near)
    near_tok = near_tok, hop(near_tok, 1)
    first_far = [m for m in far_chips if m & low_bit]
    later_far = [m for m in far_chips if not m & low_bit]
    for m in sorted(later_far):
        got[m] = hop(got[m ^ (m & -m)], m & -m)
    both = hop(jnp.stack([cross] + [got[m ^ low_bit] for m in first_far]), low_bit)
    away_near.append(both[0])
    for i, m in enumerate(first_far):
        got[m] = both[1 + i]
    far = [got[m] for m in far_chips]
    near_sums = sums_of(near_tok)
    own_in, away_near, far, near_tok, near_sums = settle(
        own_in, away_near, far, near_tok, near_sums
    )

    near_in = hop(near_sums, half)
    got = dict(zip(near_chips, away_near))
    for m in sorted(far_chips, key=lambda m: bin(m).count("1")):
        got[m] = hop(got[m ^ (m & -m)], m & -m)
    away_far = [got[m] for m in far_chips]
    mixed = jnp.stack([cross] + away_near + far)
    others = hop(mixed, 1)
    cut = 1 + len(near_chips)
    away_own_tok = mixed[:1], others[:1]
    away_near_tok = mixed[1:cut], others[1:cut]
    far_tok = mixed[cut:], others[cut:]
    far_sums = sums_of(far_tok)
    away_own_hidden = hidden_of(away_own_tok, own_in)
    weights = doubled(weights, near_chips[:-1])
    (
        near_in, away_far, away_near_tok, away_own_tok, far_tok, far_sums, away_own_hidden, weights
    ) = settle(
        near_in, away_far, away_near_tok, away_own_tok, far_tok, far_sums, away_own_hidden, weights
    )

    far_in = hop(far_sums, half)
    own_hidden = hop(away_own_hidden, half)
    away_far_tok = jnp.stack(away_far)
    away_far_tok = away_far_tok, hop(away_far_tok, 1)
    away_near_hidden = hidden_of(away_near_tok, near_in)
    away_own_rows = rows_of(away_own_tok, away_own_hidden)
    away_near_rows = rows_of(away_near_tok, away_near_hidden)
    lower = doubled(weights[:, :upper_row], group_bits, "groups")
    upper = doubled(weights[:, upper_row:], [low_bit])
    (
        far_in, own_hidden, away_far_tok, away_near_hidden, away_own_rows, away_near_rows,
        lower, upper,
    ) = settle(
        far_in, own_hidden, away_far_tok, away_near_hidden, away_own_rows, away_near_rows,
        lower, upper,
    )

    near_hidden = hop(away_near_hidden, half)
    away_others = hop(jnp.concatenate([away_own_rows[1], away_near_rows[1]]), 1)
    away_far_hidden = hidden_of(away_far_tok, far_in)
    away_far_rows = rows_of(away_far_tok, away_far_hidden)
    own_rows = rows_of(own_tok, own_hidden)
    lower = doubled(lower, [low_bit])
    upper = doubled(upper, group_bits, "groups")
    weights = jnp.concatenate([lower, upper])
    near_hidden, away_others, away_far_hidden, away_far_rows, own_rows, weights = settle(
        near_hidden, away_others, away_far_hidden, away_far_rows, own_rows, weights
    )

    far_hidden = hop(away_far_hidden, half)
    stacks = weights, hop(weights, 1)
    shared_own, shared_other = shared_sums(stacks)
    parts = hops_of(summed(away_near_rows[0], away_others[1:]), near_chips)
    others = hop(jnp.concatenate([own_rows[1], away_far_rows[1]]), 1)
    near_rows = rows_of(near_tok, near_hidden)
    far_hidden, stacks, shared_own, shared_other, parts, others, near_rows = settle(
        far_hidden, stacks, shared_own, shared_other, parts, others, near_rows
    )

    shared_in = hop(shared_own, half)
    parts += hops_of(summed(away_far_rows[0], others[1:]), far_chips)
    near_others = hop(near_rows[1], 1)
    far_rows = rows_of(far_tok, far_hidden)
    shared_in, parts, near_others, far_rows = settle(shared_in, parts, near_others, far_rows)

    total = shared_other + shared_in.astype(f32)
    other_hidden = (silu(total[:, :units]) * total[:, units:]).astype(bf16)
    shared_hidden = hop(other_hidden, half)
    shared_out = shared_down_of(other_hidden, stacks)
    away_rows = finished(shared_out, away_own_rows[0], away_others[0], parts)
    parts = hops_of(summed(near_rows[0], near_others), near_chips)
    far_others = hop(far_rows[1], 1)
    shared_hidden, away_rows, parts, far_others = settle(
        shared_hidden, away_rows, parts, far_others
    )

    far_half = hop(away_rows, half)
    parts += hops_of(summed(far_rows[0], far_others), far_chips)
    shared_out = shared_down_of(shared_hidden, stacks)
    near_half = finished(shared_out, own_rows[0], others[0], parts)
    return ordered(is_upper, near_half, far_half, 1)


def solution(mesh):
    in_specs = (
        P(("groups", "expert"), None),
        P("expert", None),
        P(None, "expert"),
        P("expert", None),
        P(None, "expert"),
        P(),
        P(("groups", "expert"), None),
        P(("groups", "expert"), None),
    )
    out_specs = P(("groups", "expert"), None)
    return jax.shard_map(local, mesh=mesh, in_specs=in_specs, out_specs=out_specs, check_vma=False)
```

```python
import functools

import jax
import jax.numpy as jnp
from jax import lax
from jax.experimental import pallas as pl
from jax.experimental.pallas import tpu as pltpu
from jax.sharding import PartitionSpec as P

route_scale = 2.5
meta_lanes = 128
vmem_bytes = 48 * 1024 * 1024
f32 = jnp.float32
bf16 = jnp.bfloat16


def hop(block, mask, axis="expert"):
    count = lax.axis_size(axis)
    return lax.ppermute(block, axis, [(d, d ^ mask) for d in range(count)])


def settle(*values):
    return lax.optimization_barrier(values)


def ordered(is_upper, own_part, other_part, axis_dim):
    return jnp.where(
        is_upper,
        jnp.concatenate([other_part, own_part], axis_dim),
        jnp.concatenate([own_part, other_part], axis_dim),
    )


def silu(v):
    return v / (1.0 + jnp.exp(-v))


def slots_of(meta, pair, lanes):
    m = meta.astype(f32)
    rows = m.shape[0]
    first = m[:, 0:1] == pair
    second = m[:, 1:2] == pair
    gate = jnp.where(first, m[:, 2:3] + m[:, 3:4], 0.0) + jnp.where(
        second, m[:, 4:5] + m[:, 5:6], 0.0
    )
    hit = jnp.where(first, 1.0, 0.0) + jnp.where(second, 1.0, 0.0)
    before = lax.broadcasted_iota(jnp.int32, (rows, rows), 1) < lax.broadcasted_iota(
        jnp.int32, (rows, rows), 0
    )
    wide_hit = jnp.broadcast_to(hit, (rows, lanes))
    rank = jnp.dot(
        jnp.where(before, 1.0, 0.0).astype(bf16), wide_hit.astype(bf16), preferred_element_type=f32
    )
    slot = lax.broadcasted_iota(jnp.int32, (rows, lanes), 1).astype(f32)
    one_hot = jnp.where(rank == slot, wide_hit, 0.0).astype(bf16)
    return one_hot, gate


def pick_rows(pair_ref, first_ref, second_ref, rows_ref, cap):
    width = rows_ref.shape[1]
    count = first_ref.shape[1]
    pair = pair_ref[0].astype(f32)
    lanes = -(-cap // 128) * 128
    dims = (((0,), (0,)), ((), ()))
    for q in range(first_ref.shape[0]):
        meta = jnp.concatenate([first_ref[q, :, width:], second_ref[q, :, width:]], 0)
        one_hot, _ = slots_of(meta, pair, lanes)
        rows = lax.dot_general(
            one_hot[:count], first_ref[q, :, :width], dims, preferred_element_type=f32
        ) + lax.dot_general(
            one_hot[count:], second_ref[q, :, :width], dims, preferred_element_type=f32
        )
        rows_ref[q * cap : (q + 1) * cap, :] = rows[:cap].astype(bf16)


def partial_kernel(cap, pair_ref, first_ref, second_ref, w_ref, out_ref, rows_ref):
    @pl.when(pl.program_id(0) == 0)
    def _():
        pick_rows(pair_ref, first_ref, second_ref, rows_ref, cap)

    out_ref[...] = jnp.dot(
        rows_ref[...], w_ref[...], preferred_element_type=f32
    ).astype(bf16)


def hidden_kernel(
    cap, pair_ref, first_ref, second_ref, wg_ref, wu_ref, rg_ref, ru_ref, out_ref, rows_ref
):
    @pl.when(pl.program_id(0) == 0)
    def _():
        pick_rows(pair_ref, first_ref, second_ref, rows_ref, cap)

    rows = rows_ref[...]
    gate = jnp.dot(rows, wg_ref[...], preferred_element_type=f32) + rg_ref[...].astype(f32)
    up = jnp.dot(rows, wu_ref[...], preferred_element_type=f32) + ru_ref[...].astype(f32)
    out_ref[...] = (silu(gate) * up).astype(bf16)


def down_kernel(
    cap,
    pair_ref,
    first_ref,
    second_ref,
    hid_ref,
    w_ref,
    near_ref,
    far_ref,
    hit_ref,
    gate_ref,
    rows_ref,
):
    chips, count, _ = near_ref.shape

    @pl.when(pl.program_id(0) == 0)
    def _():
        for q in range(chips):
            meta = jnp.concatenate([first_ref[q], second_ref[q]], 0)
            one_hot, gate = slots_of(meta, pair_ref[0].astype(f32), hit_ref.shape[2])
            hit_ref[q] = one_hot
            gate_ref[q] = jnp.broadcast_to(gate, gate_ref.shape[1:])
        rows_ref[...] = jnp.zeros_like(rows_ref)

    rows = jnp.dot(hid_ref[...], w_ref[...], preferred_element_type=f32).astype(bf16)
    for q in range(chips):
        rows_ref[q, :cap, :] = rows[q * cap : (q + 1) * cap]
        picked = jnp.dot(hit_ref[q], rows_ref[q], preferred_element_type=f32)
        gated = (picked * gate_ref[q, :, 0:1]).astype(bf16)
        near_ref[q] = gated[:count]
        far_ref[q] = gated[count:]


def params():
    return pltpu.CompilerParams(
        vmem_limit_bytes=vmem_bytes, dimension_semantics=("arbitrary",)
    )


def smem():
    return pl.BlockSpec(memory_space=pltpu.SMEM)


def whole(array):
    return pl.BlockSpec(array.shape, lambda j: (0,) * len(array.shape))


def cost(m, k, n):
    return pl.CostEstimate(flops=0, bytes_accessed=0, transcendentals=0)


def partial_sums(pair, tok, weights, cap):
    width, columns = weights.shape
    rows = tok[0].shape[0] * cap
    steps = 4
    return pl.pallas_call(
        functools.partial(partial_kernel, cap),
        grid=(steps,),
        in_specs=[
            smem(),
            whole(tok[0]),
            whole(tok[1]),
            pl.BlockSpec((width, columns // steps), lambda j: (0, j)),
        ],
        out_specs=pl.BlockSpec((rows, columns // steps), lambda j: (0, j)),
        out_shape=jax.ShapeDtypeStruct((rows, columns), bf16),
        scratch_shapes=[pltpu.VMEM((rows, width), bf16)],
        compiler_params=params(),
        cost_estimate=cost(rows, width, columns),
    )(pair, *tok, weights)


def hidden_rows(pair, tok, weights, received, cap):
    width, columns = weights.shape
    units = columns // 2
    rows = received.shape[0]
    steps = 4
    block = units // steps
    return pl.pallas_call(
        functools.partial(hidden_kernel, cap),
        grid=(steps,),
        in_specs=[
            smem(),
            whole(tok[0]),
            whole(tok[1]),
            pl.BlockSpec((width, block), lambda j: (0, j)),
            pl.BlockSpec((width, block), lambda j: (0, j + steps)),
            pl.BlockSpec((rows, block), lambda j: (0, j)),
            pl.BlockSpec((rows, block), lambda j: (0, j + steps)),
        ],
        out_specs=pl.BlockSpec((rows, block), lambda j: (0, j)),
        out_shape=jax.ShapeDtypeStruct((rows, units), bf16),
        scratch_shapes=[pltpu.VMEM((rows, width), bf16)],
        compiler_params=params(),
        cost_estimate=cost(rows, width, columns),
    )(pair, *tok, weights, weights, received, received)


def weighted_rows(pair, tok, hidden, weights, cap):
    units, width = weights.shape
    chips, count, _ = tok[0].shape
    lanes = -(-cap // 128) * 128
    steps = 2
    block = width // steps
    meta = pl.BlockSpec((chips, count, meta_lanes), lambda j: (0, 0, width // meta_lanes))
    return pl.pallas_call(
        functools.partial(down_kernel, cap),
        grid=(steps,),
        in_specs=[
            smem(),
            meta,
            meta,
            whole(hidden),
            pl.BlockSpec((units, block), lambda j: (0, j)),
        ],
        out_specs=[pl.BlockSpec((chips, count, block), lambda j: (0, 0, j))] * 2,
        out_shape=[jax.ShapeDtypeStruct((chips, count, width), bf16)] * 2,
        scratch_shapes=[
            pltpu.VMEM((chips, 2 * count, lanes), bf16),
            pltpu.VMEM((chips, 2 * count, 128), f32),
            pltpu.VMEM((chips, lanes, block), bf16),
        ],
        compiler_params=params(),
        cost_estimate=cost(chips * cap, units, width),
    )(pair, *tok, hidden, weights)


def assemble(masks, first_column, spots_ref, stack_refs, out_ref, sems):
    count = len(masks)
    columns = out_ref.shape[1] // len({q for _, _, q in masks})
    shard_rows = out_ref.shape[0] // len({m for _, m, _ in masks}) // 2
    places = [(ref, i) for ref in stack_refs for i in range(ref.shape[0])]
    copies = []
    for at, (stack_ref, i) in enumerate(places):
        upper, _, q = masks[at % count]
        rows = stack_ref.shape[1]
        row = pl.multiple_of(spots_ref[at] * shard_rows + upper * rows, rows)
        column = pl.multiple_of(spots_ref[2 * count + q] * columns, columns)
        copies.append(
            pltpu.make_async_copy(
                stack_ref.at[i, :, pl.ds(first_column, columns)],
                out_ref.at[pl.ds(row, rows), pl.ds(column, columns)],
                sems.at[at],
            )
        )
    for copy in copies:
        copy.start()
    for copy in copies:
        copy.wait()


def shared_gate_kernel(masks, spots_ref, own_ref, other_ref, *refs):
    stack_refs, (mine_ref, theirs_ref, w_ref, sems) = refs[:-4], refs[-4:]
    assemble(masks, 0, spots_ref, stack_refs, w_ref, sems)
    width, columns = w_ref.shape
    step = 512

    @pl.loop(0, columns // step)
    def _(j):
        at = pl.ds(pl.multiple_of(j * step, step), step)
        w = w_ref[:, at]
        mine_ref[:, at] = jnp.dot(own_ref[:, :width], w, preferred_element_type=f32).astype(bf16)
        theirs_ref[:, at] = jnp.dot(other_ref[:, :width], w, preferred_element_type=f32)


def shared_partial(spots, masks, own, other, stacks, width, columns):
    rows = own.shape[0]
    vmem = pl.BlockSpec(memory_space=pltpu.VMEM)
    hbm = pl.BlockSpec(memory_space=pl.ANY)
    return pl.pallas_call(
        functools.partial(shared_gate_kernel, masks),
        in_specs=[smem(), vmem, vmem] + [hbm] * len(stacks),
        out_specs=[vmem, vmem],
        out_shape=[
            jax.ShapeDtypeStruct((rows, columns), bf16),
            jax.ShapeDtypeStruct((rows, columns), f32),
        ],
        scratch_shapes=[
            pltpu.VMEM((width, columns), bf16),
            pltpu.SemaphoreType.DMA((2 * len(masks),)),
        ],
        compiler_params=pltpu.CompilerParams(vmem_limit_bytes=vmem_bytes),
        cost_estimate=cost(2 * rows, width, columns),
    )(spots, own, other, *stacks)


def shared_down_kernel(masks, first_column, spots_ref, hid_ref, *refs):
    stack_refs, (out_ref, d_ref, sems) = refs[:-3], refs[-3:]
    assemble(masks, first_column, spots_ref, stack_refs, d_ref, sems)
    step = 256

    @pl.loop(0, d_ref.shape[0] // step)
    def _(j):
        at = pl.ds(pl.multiple_of(j * step, step), step)
        out_ref[:, at] = lax.dot_general(
            hid_ref[...], d_ref[at, :], (((1,), (1,)), ((), ())), preferred_element_type=f32
        ).astype(bf16)


def shared_rows(spots, masks, hidden, stacks, first_column, width):
    rows, units = hidden.shape
    vmem = pl.BlockSpec(memory_space=pltpu.VMEM)
    hbm = pl.BlockSpec(memory_space=pl.ANY)
    return pl.pallas_call(
        functools.partial(shared_down_kernel, masks, first_column),
        in_specs=[smem(), vmem] + [hbm] * len(stacks),
        out_specs=vmem,
        out_shape=jax.ShapeDtypeStruct((rows, width), bf16),
        scratch_shapes=[
            pltpu.VMEM((width, units), bf16),
            pltpu.SemaphoreType.DMA((2 * len(masks),)),
        ],
        compiler_params=pltpu.CompilerParams(vmem_limit_bytes=vmem_bytes),
        cost_estimate=cost(rows, units, width),
    )(spots, hidden, *stacks)


def in_order(masks, place, group_index, stacks):
    groups = len({q for _, _, q in masks})
    shards = 2 * len({m for _, m, _ in masks})
    rows = min(stack.shape[1] for stack in stacks)
    pieces = [
        (stack[i : i + 1, at : at + rows], i_mask, stack.shape[1] > rows and at > 0)
        for stack, i, i_mask in numbered(masks, stacks)
        for at in range(0, stack.shape[1], rows)
    ]
    spot = {}
    for number, (_, (core, upper, m, q), second) in enumerate(pieces):
        spot[m | core, 1 if second else upper, q] = number
    table = [[[spot[m, u, q] for q in range(groups)] for u in (0, 1)] for m in range(shards)]
    table = jnp.array(table, jnp.int32)
    table = table[jnp.arange(shards, dtype=jnp.int32) ^ place]
    table = table[:, :, jnp.arange(groups, dtype=jnp.int32) ^ group_index]
    parts = jnp.concatenate([piece for piece, _, _ in pieces])[table]
    parts = parts.transpose(0, 1, 3, 2, 4)
    return parts.reshape(shards, -1, groups, parts.shape[-1])


def numbered(masks, stacks):
    places = [(stack, i) for stack in stacks for i in range(stack.shape[0])]
    count = len(masks)
    return [
        (stack, i, (at // count,) + masks[at % count]) for at, (stack, i) in enumerate(places)
    ]


def local(
    tokens,
    expert_gate_up,
    expert_down,
    shared_gate_up,
    shared_down,
    host_expert,
    pair_picks,
    affinity,
):
    devices = lax.axis_size("expert")
    groups = lax.axis_size("groups")
    half = devices // 2
    dev_index = lax.axis_index("expert")
    group_index = lax.axis_index("groups")
    is_upper = dev_index >= half
    pair = jnp.reshape(dev_index % half, (1,)).astype(jnp.int32)
    tok_rows, full_width = tokens.shape
    width = full_width // 2
    units = expert_down.shape[0]
    pick_count = pair_picks.shape[1]
    capacity = 7 * tok_rows * pick_count // (4 * half)
    cap = -(-2 * capacity // 16) * 16
    chips = list(range(2, half, 2))
    near_chips = sorted([m for m in chips if m & (m - 1) == 0], reverse=True)
    far_chips = [m for m in chips if m & (m - 1)]

    pair_iota = jnp.arange(half, dtype=jnp.int32)
    expert_ids = jnp.sum(
        jnp.where(pair_picks[:, :, None] == pair_iota, host_expert[None, None, :], 0), 2
    )
    scores = jnp.sum(
        jnp.where(expert_ids[:, :, None] == pair_iota, affinity[:, None, :], 0.0), 2
    )
    gates = route_scale * scores / jnp.sum(scores, 1, keepdims=True)
    gates_high = lax.reduce_precision(gates, 8, 7)
    gates_low = gates - gates_high
    meta = jnp.concatenate(
        [
            pair_picks.astype(f32),
            jnp.stack([gates_high, gates_low], 2).reshape(tok_rows, 2 * pick_count),
            jnp.zeros((tok_rows, meta_lanes - 3 * pick_count), f32),
        ],
        1,
    ).astype(bf16)
    low, high = tokens[:, :width], tokens[:, width:]
    mine = jnp.concatenate([jnp.where(is_upper, high, low), meta], 1)
    theirs = jnp.concatenate([jnp.where(is_upper, low, high), meta], 1)

    def sums_of(tok):
        return partial_sums(pair, tok, expert_gate_up, cap)

    def hidden_of(tok, sums):
        return hidden_rows(pair, tok, expert_gate_up, sums, cap)

    def rows_of(tok, hidden):
        return weighted_rows(pair, tok, hidden, expert_down, cap)

    def summed(rows, other):
        return (rows.astype(f32) + other.astype(f32)).astype(bf16)

    def hops_of(blocks, masks):
        return [hop(block, m) for m, block in zip(masks, blocks)]

    def finished(shared, rows, other, parts):
        total = shared.astype(f32) + rows[0].astype(f32) + other.astype(f32)
        for part in parts:
            total = total + part.astype(f32)
        return total.astype(bf16)

    low_bit, later_bits = near_chips[-1], near_chips[:-1]
    group_bits = [1 << i for i in range(groups.bit_length() - 1)]
    gate_columns = 2 * units // groups
    down_rows = units // groups
    shard_rows = shared_gate_up.shape[0]
    upper_row = shard_rows // 2

    def share_of_weights():
        gate = lax.dynamic_slice_in_dim(shared_gate_up, group_index * gate_columns, gate_columns, 1)
        down = lax.dynamic_slice_in_dim(shared_down, group_index * down_rows, down_rows, 0)
        return jnp.concatenate([gate, down.T], 1)[None]

    def doubled(stack, bits, axis="expert"):
        for bit in bits:
            stack = jnp.concatenate([stack, hop(stack, bit, axis)])
        return stack

    def masks_of(upper, steps):
        masks = [(0, 0)]
        for m, q in steps:
            masks = masks + [(a ^ m, b ^ q) for a, b in masks]
        return [(upper, a, b) for a, b in masks]

    start_masks = masks_of(0, [(m, 0) for m in later_bits])
    all_groups = masks_of(0, [(m, 0) for m in later_bits] + [(0, q) for q in group_bits])
    other_groups = all_groups[len(start_masks) :]
    masks = start_masks + other_groups + [(0, m ^ low_bit, q) for _, m, q in start_masks]
    masks += [(upper, m ^ low_bit, q) for upper in (0, 1) for _, m, q in other_groups]
    place = dev_index % half
    chip_masks = jnp.array([m for _, m, _ in masks], jnp.int32)
    spots = jnp.concatenate(
        [place ^ chip_masks, place ^ 1 ^ chip_masks, group_index ^ jnp.arange(groups)]
    ).astype(jnp.int32)
    by_kernel = upper_row % 16 == 0

    def shared_sums(stacks):
        if by_kernel:
            return shared_partial(spots, masks, mine, cross, stacks, width, 2 * units)
        gate = in_order(masks, place, group_index, stacks)[..., :gate_columns]
        gate = gate.reshape(width, 2 * units)
        own = jnp.dot(mine[:, :width], gate, preferred_element_type=f32).astype(bf16)
        return own, jnp.dot(cross[:, :width], gate, preferred_element_type=f32)

    def shared_down_of(hidden, stacks):
        if by_kernel:
            return shared_rows(spots, masks, hidden, stacks, gate_columns, width)
        down = in_order(masks, place, group_index, stacks)[..., gate_columns:]
        down = down.reshape(width, units)
        return lax.dot_general(
            hidden, down, (((1,), (1,)), ((), ())), preferred_element_type=f32
        ).astype(bf16)

    cross = hop(theirs, half)
    near = [hop(mine, m) for m in near_chips]
    own_tok = mine[None], hop(mine, 1)[None]
    own_sums = sums_of(own_tok)
    weights = share_of_weights()
    cross, near, own_tok, own_sums, weights = settle(cross, near, own_tok, own_sums, weights)

    own_in = hop(own_sums, half)
    got = dict(zip(near_chips, near))
    away_near = [hop(cross, m) for m in near_chips[:-1]]
    near_tok = jnp.stack(near)
    near_tok = near_tok, hop(near_tok, 1)
    first_far = [m for m in far_chips if m & low_bit]
    later_far = [m for m in far_chips if not m & low_bit]
    for m in sorted(later_far):
        got[m] = hop(got[m ^ (m & -m)], m & -m)
    both = hop(jnp.stack([cross] + [got[m ^ low_bit] for m in first_far]), low_bit)
    away_near.append(both[0])
    for i, m in enumerate(first_far):
        got[m] = both[1 + i]
    far = [got[m] for m in far_chips]
    near_sums = sums_of(near_tok)
    own_in, away_near, far, near_tok, near_sums = settle(
        own_in, away_near, far, near_tok, near_sums
    )

    near_in = hop(near_sums, half)
    got = dict(zip(near_chips, away_near))
    for m in sorted(far_chips, key=lambda m: bin(m).count("1")):
        got[m] = hop(got[m ^ (m & -m)], m & -m)
    away_far = [got[m] for m in far_chips]
    mixed = jnp.stack([cross] + away_near + far)
    others = hop(mixed, 1)
    cut = 1 + len(near_chips)
    away_own_tok = mixed[:1], others[:1]
    away_near_tok = mixed[1:cut], others[1:cut]
    far_tok = mixed[cut:], others[cut:]
    far_sums = sums_of(far_tok)
    away_own_hidden = hidden_of(away_own_tok, own_in)
    weights = doubled(weights, later_bits)
    (
        near_in, away_far, away_near_tok, away_own_tok, far_tok, far_sums, away_own_hidden, weights
    ) = settle(
        near_in, away_far, away_near_tok, away_own_tok, far_tok, far_sums, away_own_hidden, weights
    )

    far_in = hop(far_sums, half)
    own_hidden = hop(away_own_hidden, half)
    away_far_tok = jnp.stack(away_far)
    away_far_tok = away_far_tok, hop(away_far_tok, 1)
    away_near_hidden = hidden_of(away_near_tok, near_in)
    away_own_rows = rows_of(away_own_tok, away_own_hidden)
    away_near_rows = rows_of(away_near_tok, away_near_hidden)
    by_group = doubled(weights, group_bits, "groups")[weights.shape[0] :]
    by_chip = hop(weights, low_bit)
    (
        far_in, own_hidden, away_far_tok, away_near_hidden, away_own_rows, away_near_rows,
        by_group, by_chip,
    ) = settle(
        far_in, own_hidden, away_far_tok, away_near_hidden, away_own_rows, away_near_rows,
        by_group, by_chip,
    )

    near_hidden = hop(away_near_hidden, half)
    away_others = hop(jnp.concatenate([away_own_rows[1], away_near_rows[1]]), 1)
    lower = hop(by_group[:, :upper_row], low_bit)
    upper = doubled(by_chip[:, upper_row:], group_bits, "groups")[by_chip.shape[0] :]
    first = jnp.concatenate([weights, by_group, by_chip])
    first_other = hop(first, 1)
    far_in, own_hidden, away_others = settle(far_in, own_hidden, away_others)
    away_far_hidden = hidden_of(away_far_tok, far_in)
    away_far_rows = rows_of(away_far_tok, away_far_hidden)
    own_rows = rows_of(own_tok, own_hidden)
    (
        near_hidden, away_others, away_far_hidden, away_far_rows, own_rows, first, first_other,
        lower, upper,
    ) = settle(
        near_hidden, away_others, away_far_hidden, away_far_rows, own_rows, first, first_other,
        lower, upper,
    )

    far_hidden = hop(away_far_hidden, half)
    second = jnp.concatenate([lower, upper])
    stacks = first, second, first_other, hop(second, 1)
    shared_own, shared_other = shared_sums(stacks)
    near_hidden, shared_own = settle(near_hidden, shared_own)
    parts = hops_of(summed(away_near_rows[0], away_others[1:]), near_chips)
    others = hop(jnp.concatenate([own_rows[1], away_far_rows[1]]), 1)
    near_rows = rows_of(near_tok, near_hidden)
    far_hidden, stacks, shared_own, shared_other, parts, others, near_rows = settle(
        far_hidden, stacks, shared_own, shared_other, parts, others, near_rows
    )

    shared_in = hop(shared_own, half)
    parts += hops_of(summed(away_far_rows[0], others[1:]), far_chips)
    near_others = hop(near_rows[1], 1)
    far_rows = rows_of(far_tok, far_hidden)
    shared_in, parts, near_others, far_rows = settle(shared_in, parts, near_others, far_rows)

    total = shared_other + shared_in.astype(f32)
    other_hidden = (silu(total[:, :units]) * total[:, units:]).astype(bf16)
    shared_hidden = hop(other_hidden, half)
    shared_out = shared_down_of(other_hidden, stacks)
    away_rows = finished(shared_out, away_own_rows[0], away_others[0], parts)
    parts = hops_of(summed(near_rows[0], near_others), near_chips)
    far_others = hop(far_rows[1], 1)
    far_half = hop(away_rows, half)
    shared_hidden, parts[-1] = settle(shared_hidden, parts[-1])
    parts += hops_of(summed(far_rows[0], far_others), far_chips)
    shared_out = shared_down_of(shared_hidden, stacks)
    near_half = finished(shared_out, own_rows[0], others[0], parts)
    return ordered(is_upper, near_half, far_half, 1)


def solution(mesh):
    in_specs = (
        P(("groups", "expert"), None),
        P("expert", None),
        P(None, "expert"),
        P("expert", None),
        P(None, "expert"),
        P(),
        P(("groups", "expert"), None),
        P(("groups", "expert"), None),
    )
    out_specs = P(("groups", "expert"), None)
    return jax.shard_map(local, mesh=mesh, in_specs=in_specs, out_specs=out_specs, check_vma=False)
```

```python
import functools

import jax
import jax.numpy as jnp
from jax import lax
from jax.experimental import pallas as pl
from jax.experimental.pallas import tpu as pltpu
from jax.sharding import PartitionSpec as P

route_scale = 2.5
meta_lanes = 128
vmem_bytes = 48 * 1024 * 1024
f32 = jnp.float32
bf16 = jnp.bfloat16


def hop(block, mask, axis="expert"):
    count = lax.axis_size(axis)
    return lax.ppermute(block, axis, [(d, d ^ mask) for d in range(count)])


def settle_round(late, *values):
    last, rest = values[:late], lax.optimization_barrier(values[late:])
    last, rest = lax.optimization_barrier((last, rest))
    return last + rest


def settle(*values):
    return lax.optimization_barrier(values)


def ordered(is_upper, own_part, other_part, axis_dim):
    return jnp.where(
        is_upper,
        jnp.concatenate([other_part, own_part], axis_dim),
        jnp.concatenate([own_part, other_part], axis_dim),
    )


def silu(v):
    return v / (1.0 + jnp.exp(-v))


def slots_of(meta, pair, lanes):
    m = meta.astype(f32)
    rows = m.shape[0]
    first = m[:, 0:1] == pair
    second = m[:, 1:2] == pair
    gate = jnp.where(first, m[:, 2:3] + m[:, 3:4], 0.0) + jnp.where(
        second, m[:, 4:5] + m[:, 5:6], 0.0
    )
    hit = jnp.where(first, 1.0, 0.0) + jnp.where(second, 1.0, 0.0)
    before = lax.broadcasted_iota(jnp.int32, (rows, rows), 1) < lax.broadcasted_iota(
        jnp.int32, (rows, rows), 0
    )
    wide_hit = jnp.broadcast_to(hit, (rows, lanes))
    rank = jnp.dot(
        jnp.where(before, 1.0, 0.0).astype(bf16), wide_hit.astype(bf16), preferred_element_type=f32
    )
    slot = lax.broadcasted_iota(jnp.int32, (rows, lanes), 1).astype(f32)
    one_hot = jnp.where(rank == slot, wide_hit, 0.0).astype(bf16)
    return one_hot, gate


def pick_rows(pair_ref, first_ref, second_ref, rows_ref, cap):
    width = rows_ref.shape[1]
    count = first_ref.shape[1]
    pair = pair_ref[0].astype(f32)
    lanes = -(-cap // 128) * 128
    dims = (((0,), (0,)), ((), ()))
    for q in range(first_ref.shape[0]):
        meta = jnp.concatenate([first_ref[q, :, width:], second_ref[q, :, width:]], 0)
        one_hot, _ = slots_of(meta, pair, lanes)
        rows = lax.dot_general(
            one_hot[:count], first_ref[q, :, :width], dims, preferred_element_type=f32
        ) + lax.dot_general(
            one_hot[count:], second_ref[q, :, :width], dims, preferred_element_type=f32
        )
        rows_ref[q * cap : (q + 1) * cap, :] = rows[:cap].astype(bf16)


def partial_kernel(cap, pair_ref, first_ref, second_ref, w_ref, out_ref, rows_ref):
    @pl.when(pl.program_id(0) == 0)
    def _():
        pick_rows(pair_ref, first_ref, second_ref, rows_ref, cap)

    out_ref[...] = jnp.dot(
        rows_ref[...], w_ref[...], preferred_element_type=f32
    ).astype(bf16)


def hidden_kernel(
    cap, pair_ref, first_ref, second_ref, wg_ref, wu_ref, rg_ref, ru_ref, out_ref, rows_ref
):
    @pl.when(pl.program_id(0) == 0)
    def _():
        pick_rows(pair_ref, first_ref, second_ref, rows_ref, cap)

    rows = rows_ref[...]
    gate = jnp.dot(rows, wg_ref[...], preferred_element_type=f32) + rg_ref[...].astype(f32)
    up = jnp.dot(rows, wu_ref[...], preferred_element_type=f32) + ru_ref[...].astype(f32)
    out_ref[...] = (silu(gate) * up).astype(bf16)


def down_kernel(
    cap,
    pair_ref,
    first_ref,
    second_ref,
    hid_ref,
    w_ref,
    near_ref,
    far_ref,
    hit_ref,
    gate_ref,
    rows_ref,
):
    chips, count, _ = near_ref.shape

    @pl.when(pl.program_id(0) == 0)
    def _():
        for q in range(chips):
            meta = jnp.concatenate([first_ref[q], second_ref[q]], 0)
            one_hot, gate = slots_of(meta, pair_ref[0].astype(f32), hit_ref.shape[2])
            hit_ref[q] = one_hot
            gate_ref[q] = jnp.broadcast_to(gate, gate_ref.shape[1:])
        rows_ref[...] = jnp.zeros_like(rows_ref)

    rows = jnp.dot(hid_ref[...], w_ref[...], preferred_element_type=f32).astype(bf16)
    for q in range(chips):
        rows_ref[q, :cap, :] = rows[q * cap : (q + 1) * cap]
        picked = jnp.dot(hit_ref[q], rows_ref[q], preferred_element_type=f32)
        gated = (picked * gate_ref[q, :, 0:1]).astype(bf16)
        near_ref[q] = gated[:count]
        far_ref[q] = gated[count:]


def params():
    return pltpu.CompilerParams(
        vmem_limit_bytes=vmem_bytes, dimension_semantics=("arbitrary",)
    )


def smem():
    return pl.BlockSpec(memory_space=pltpu.SMEM)


def whole(array):
    return pl.BlockSpec(array.shape, lambda j: (0,) * len(array.shape))


def cost(m, k, n):
    return pl.CostEstimate(flops=0, bytes_accessed=0, transcendentals=0)


def partial_sums(pair, tok, weights, cap):
    width, columns = weights.shape
    rows = tok[0].shape[0] * cap
    steps = 4
    return pl.pallas_call(
        functools.partial(partial_kernel, cap),
        grid=(steps,),
        in_specs=[
            smem(),
            whole(tok[0]),
            whole(tok[1]),
            pl.BlockSpec((width, columns // steps), lambda j: (0, j)),
        ],
        out_specs=pl.BlockSpec((rows, columns // steps), lambda j: (0, j)),
        out_shape=jax.ShapeDtypeStruct((rows, columns), bf16),
        scratch_shapes=[pltpu.VMEM((rows, width), bf16)],
        compiler_params=params(),
        cost_estimate=cost(rows, width, columns),
    )(pair, *tok, weights)


def hidden_rows(pair, tok, weights, received, cap):
    width, columns = weights.shape
    units = columns // 2
    rows = received.shape[0]
    steps = 4
    block = units // steps
    return pl.pallas_call(
        functools.partial(hidden_kernel, cap),
        grid=(steps,),
        in_specs=[
            smem(),
            whole(tok[0]),
            whole(tok[1]),
            pl.BlockSpec((width, block), lambda j: (0, j)),
            pl.BlockSpec((width, block), lambda j: (0, j + steps)),
            pl.BlockSpec((rows, block), lambda j: (0, j)),
            pl.BlockSpec((rows, block), lambda j: (0, j + steps)),
        ],
        out_specs=pl.BlockSpec((rows, block), lambda j: (0, j)),
        out_shape=jax.ShapeDtypeStruct((rows, units), bf16),
        scratch_shapes=[pltpu.VMEM((rows, width), bf16)],
        compiler_params=params(),
        cost_estimate=cost(rows, width, columns),
    )(pair, *tok, weights, weights, received, received)


def weighted_rows(pair, tok, hidden, weights, cap):
    units, width = weights.shape
    chips, count, _ = tok[0].shape
    lanes = -(-cap // 128) * 128
    steps = 2
    block = width // steps
    meta = pl.BlockSpec((chips, count, meta_lanes), lambda j: (0, 0, width // meta_lanes))
    return pl.pallas_call(
        functools.partial(down_kernel, cap),
        grid=(steps,),
        in_specs=[
            smem(),
            meta,
            meta,
            whole(hidden),
            pl.BlockSpec((units, block), lambda j: (0, j)),
        ],
        out_specs=[pl.BlockSpec((chips, count, block), lambda j: (0, 0, j))] * 2,
        out_shape=[jax.ShapeDtypeStruct((chips, count, width), bf16)] * 2,
        scratch_shapes=[
            pltpu.VMEM((chips, 2 * count, lanes), bf16),
            pltpu.VMEM((chips, 2 * count, 128), f32),
            pltpu.VMEM((chips, lanes, block), bf16),
        ],
        compiler_params=params(),
        cost_estimate=cost(chips * cap, units, width),
    )(pair, *tok, hidden, weights)


def assemble(masks, first_column, spots_ref, stack_refs, out_ref, sems):
    count = len(masks)
    columns = out_ref.shape[1] // len({q for _, _, q in masks})
    shard_rows = out_ref.shape[0] // len({m for _, m, _ in masks}) // 2
    places = [(ref, i) for ref in stack_refs for i in range(ref.shape[0])]
    copies = []
    for at, (stack_ref, i) in enumerate(places):
        upper, _, q = masks[at % count]
        rows = stack_ref.shape[1]
        row = pl.multiple_of(spots_ref[at] * shard_rows + upper * rows, rows)
        column = pl.multiple_of(spots_ref[2 * count + q] * columns, columns)
        copies.append(
            pltpu.make_async_copy(
                stack_ref.at[i, :, pl.ds(first_column, columns)],
                out_ref.at[pl.ds(row, rows), pl.ds(column, columns)],
                sems.at[at],
            )
        )
    for copy in copies:
        copy.start()
    for copy in copies:
        copy.wait()


def shared_gate_kernel(masks, spots_ref, own_ref, other_ref, *refs):
    stack_refs, (mine_ref, theirs_ref, w_ref, sems) = refs[:-4], refs[-4:]
    assemble(masks, 0, spots_ref, stack_refs, w_ref, sems)
    width, columns = w_ref.shape
    step = 512

    @pl.loop(0, columns // step)
    def _(j):
        at = pl.ds(pl.multiple_of(j * step, step), step)
        w = w_ref[:, at]
        mine_ref[:, at] = jnp.dot(own_ref[:, :width], w, preferred_element_type=f32).astype(bf16)
        theirs_ref[:, at] = jnp.dot(other_ref[:, :width], w, preferred_element_type=f32)


def shared_partial(spots, masks, own, other, stacks, width, columns):
    rows = own.shape[0]
    vmem = pl.BlockSpec(memory_space=pltpu.VMEM)
    hbm = pl.BlockSpec(memory_space=pl.ANY)
    return pl.pallas_call(
        functools.partial(shared_gate_kernel, masks),
        in_specs=[smem(), vmem, vmem] + [hbm] * len(stacks),
        out_specs=[vmem, vmem],
        out_shape=[
            jax.ShapeDtypeStruct((rows, columns), bf16),
            jax.ShapeDtypeStruct((rows, columns), f32),
        ],
        scratch_shapes=[
            pltpu.VMEM((width, columns), bf16),
            pltpu.SemaphoreType.DMA((2 * len(masks),)),
        ],
        compiler_params=pltpu.CompilerParams(vmem_limit_bytes=vmem_bytes),
        cost_estimate=cost(2 * rows, width, columns),
    )(spots, own, other, *stacks)


def shared_down_kernel(masks, first_column, spots_ref, hid_ref, *refs):
    stack_refs, (out_ref, d_ref, sems) = refs[:-3], refs[-3:]
    assemble(masks, first_column, spots_ref, stack_refs, d_ref, sems)
    step = 256

    @pl.loop(0, d_ref.shape[0] // step)
    def _(j):
        at = pl.ds(pl.multiple_of(j * step, step), step)
        out_ref[:, at] = lax.dot_general(
            hid_ref[...], d_ref[at, :], (((1,), (1,)), ((), ())), preferred_element_type=f32
        ).astype(bf16)


def shared_rows(spots, masks, hidden, stacks, first_column, width):
    rows, units = hidden.shape
    vmem = pl.BlockSpec(memory_space=pltpu.VMEM)
    hbm = pl.BlockSpec(memory_space=pl.ANY)
    return pl.pallas_call(
        functools.partial(shared_down_kernel, masks, first_column),
        in_specs=[smem(), vmem] + [hbm] * len(stacks),
        out_specs=vmem,
        out_shape=jax.ShapeDtypeStruct((rows, width), bf16),
        scratch_shapes=[
            pltpu.VMEM((width, units), bf16),
            pltpu.SemaphoreType.DMA((2 * len(masks),)),
        ],
        compiler_params=pltpu.CompilerParams(vmem_limit_bytes=vmem_bytes),
        cost_estimate=cost(rows, units, width),
    )(spots, hidden, *stacks)


def in_order(masks, place, group_index, stacks):
    groups = len({q for _, _, q in masks})
    shards = 2 * len({m for _, m, _ in masks})
    rows = min(stack.shape[1] for stack in stacks)
    pieces = [
        (stack[i : i + 1, at : at + rows], i_mask, stack.shape[1] > rows and at > 0)
        for stack, i, i_mask in numbered(masks, stacks)
        for at in range(0, stack.shape[1], rows)
    ]
    spot = {}
    for number, (_, (core, upper, m, q), second) in enumerate(pieces):
        spot[m | core, 1 if second else upper, q] = number
    table = [[[spot[m, u, q] for q in range(groups)] for u in (0, 1)] for m in range(shards)]
    table = jnp.array(table, jnp.int32)
    table = table[jnp.arange(shards, dtype=jnp.int32) ^ place]
    table = table[:, :, jnp.arange(groups, dtype=jnp.int32) ^ group_index]
    parts = jnp.concatenate([piece for piece, _, _ in pieces])[table]
    parts = parts.transpose(0, 1, 3, 2, 4)
    return parts.reshape(shards, -1, groups, parts.shape[-1])


def numbered(masks, stacks):
    places = [(stack, i) for stack in stacks for i in range(stack.shape[0])]
    count = len(masks)
    return [
        (stack, i, (at // count,) + masks[at % count]) for at, (stack, i) in enumerate(places)
    ]


def local(
    tokens,
    expert_gate_up,
    expert_down,
    shared_gate_up,
    shared_down,
    host_expert,
    pair_picks,
    affinity,
):
    devices = lax.axis_size("expert")
    groups = lax.axis_size("groups")
    half = devices // 2
    dev_index = lax.axis_index("expert")
    group_index = lax.axis_index("groups")
    is_upper = dev_index >= half
    pair = jnp.reshape(dev_index % half, (1,)).astype(jnp.int32)
    tok_rows, full_width = tokens.shape
    width = full_width // 2
    units = expert_down.shape[0]
    pick_count = pair_picks.shape[1]
    capacity = 7 * tok_rows * pick_count // (4 * half)
    cap = -(-2 * capacity // 16) * 16
    chips = list(range(2, half, 2))
    near_chips = sorted([m for m in chips if m & (m - 1) == 0], reverse=True)
    far_chips = [m for m in chips if m & (m - 1)]

    pair_iota = jnp.arange(half, dtype=jnp.int32)
    expert_ids = jnp.sum(
        jnp.where(pair_picks[:, :, None] == pair_iota, host_expert[None, None, :], 0), 2
    )
    scores = jnp.sum(
        jnp.where(expert_ids[:, :, None] == pair_iota, affinity[:, None, :], 0.0), 2
    )
    gates = route_scale * scores / jnp.sum(scores, 1, keepdims=True)
    gates_high = lax.reduce_precision(gates, 8, 7)
    gates_low = gates - gates_high
    meta = jnp.concatenate(
        [
            pair_picks.astype(f32),
            jnp.stack([gates_high, gates_low], 2).reshape(tok_rows, 2 * pick_count),
            jnp.zeros((tok_rows, meta_lanes - 3 * pick_count), f32),
        ],
        1,
    ).astype(bf16)
    low, high = tokens[:, :width], tokens[:, width:]
    mine = jnp.concatenate([jnp.where(is_upper, high, low), meta], 1)
    theirs = jnp.concatenate([jnp.where(is_upper, low, high), meta], 1)

    def sums_of(tok):
        return partial_sums(pair, tok, expert_gate_up, cap)

    def hidden_of(tok, sums):
        return hidden_rows(pair, tok, expert_gate_up, sums, cap)

    def rows_of(tok, hidden):
        return weighted_rows(pair, tok, hidden, expert_down, cap)

    def summed(rows, other):
        return (rows.astype(f32) + other.astype(f32)).astype(bf16)

    def hops_of(blocks, masks):
        return [hop(block, m) for m, block in zip(masks, blocks)]

    def finished(shared, rows, other, parts):
        total = shared.astype(f32) + rows[0].astype(f32) + other.astype(f32)
        for part in parts:
            total = total + part.astype(f32)
        return total.astype(bf16)

    low_bit, later_bits = near_chips[-1], near_chips[:-1]
    group_bits = [1 << i for i in range(groups.bit_length() - 1)]
    gate_columns = 2 * units // groups
    down_rows = units // groups
    shard_rows = shared_gate_up.shape[0]
    upper_row = shard_rows // 2

    def share_of_weights():
        gate = lax.dynamic_slice_in_dim(shared_gate_up, group_index * gate_columns, gate_columns, 1)
        down = lax.dynamic_slice_in_dim(shared_down, group_index * down_rows, down_rows, 0)
        return jnp.concatenate([gate, down.T], 1)[None]

    def doubled(stack, bits, axis="expert"):
        for bit in bits:
            stack = jnp.concatenate([stack, hop(stack, bit, axis)])
        return stack

    def masks_of(upper, steps):
        masks = [(0, 0)]
        for m, q in steps:
            masks = masks + [(a ^ m, b ^ q) for a, b in masks]
        return [(upper, a, b) for a, b in masks]

    start_masks = masks_of(0, [(m, 0) for m in later_bits])
    all_groups = masks_of(0, [(m, 0) for m in later_bits] + [(0, q) for q in group_bits])
    other_groups = all_groups[len(start_masks) :]
    masks = start_masks + other_groups + [(0, m ^ low_bit, q) for _, m, q in start_masks]
    masks += [(upper, m ^ low_bit, q) for upper in (0, 1) for _, m, q in other_groups]
    place = dev_index % half
    chip_masks = jnp.array([m for _, m, _ in masks], jnp.int32)
    spots = jnp.concatenate(
        [place ^ chip_masks, place ^ 1 ^ chip_masks, group_index ^ jnp.arange(groups)]
    ).astype(jnp.int32)
    by_kernel = upper_row % 16 == 0

    def shared_sums(stacks):
        if by_kernel:
            return shared_partial(spots, masks, mine, cross, stacks, width, 2 * units)
        gate = in_order(masks, place, group_index, stacks)[..., :gate_columns]
        gate = gate.reshape(width, 2 * units)
        own = jnp.dot(mine[:, :width], gate, preferred_element_type=f32).astype(bf16)
        return own, jnp.dot(cross[:, :width], gate, preferred_element_type=f32)

    def shared_down_of(hidden, stacks):
        if by_kernel:
            return shared_rows(spots, masks, hidden, stacks, gate_columns, width)
        down = in_order(masks, place, group_index, stacks)[..., gate_columns:]
        down = down.reshape(width, units)
        return lax.dot_general(
            hidden, down, (((1,), (1,)), ((), ())), preferred_element_type=f32
        ).astype(bf16)

    cross = hop(theirs, half)
    near = [hop(mine, m) for m in near_chips]
    own_tok = mine[None], hop(mine, 1)[None]
    own_sums = sums_of(own_tok)
    weights = share_of_weights()
    cross, near, own_tok, own_sums, weights = settle(cross, near, own_tok, own_sums, weights)

    own_in = hop(own_sums, half)
    got = dict(zip(near_chips, near))
    away_near = [hop(cross, m) for m in near_chips[:-1]]
    near_tok = jnp.stack(near)
    near_tok = near_tok, hop(near_tok, 1)
    first_far = [m for m in far_chips if m & low_bit]
    later_far = [m for m in far_chips if not m & low_bit]
    for m in sorted(later_far):
        got[m] = hop(got[m ^ (m & -m)], m & -m)
    both = hop(jnp.stack([cross] + [got[m ^ low_bit] for m in first_far]), low_bit)
    away_near.append(both[0])
    for i, m in enumerate(first_far):
        got[m] = both[1 + i]
    far = [got[m] for m in far_chips]
    near_sums = sums_of(near_tok)
    own_in, away_near, far, near_tok, near_sums = settle(
        own_in, away_near, far, near_tok, near_sums
    )

    near_in = hop(near_sums, half)
    got = dict(zip(near_chips, away_near))
    for m in sorted(far_chips, key=lambda m: bin(m).count("1")):
        got[m] = hop(got[m ^ (m & -m)], m & -m)
    away_far = [got[m] for m in far_chips]
    mixed = jnp.stack([cross] + away_near + far)
    others = hop(mixed, 1)
    cut = 1 + len(near_chips)
    away_own_tok = mixed[:1], others[:1]
    away_near_tok = mixed[1:cut], others[1:cut]
    far_tok = mixed[cut:], others[cut:]
    far_sums = sums_of(far_tok)
    away_own_hidden = hidden_of(away_own_tok, own_in)
    weights = doubled(weights, later_bits)
    (
        near_in, away_far, away_near_tok, away_own_tok, far_tok, far_sums, away_own_hidden, weights
    ) = settle(
        near_in, away_far, away_near_tok, away_own_tok, far_tok, far_sums, away_own_hidden, weights
    )

    far_in = hop(far_sums, half)
    own_hidden = hop(away_own_hidden, half)
    away_far_tok = jnp.stack(away_far)
    away_far_tok = away_far_tok, hop(away_far_tok, 1)
    away_near_hidden = hidden_of(away_near_tok, near_in)
    away_own_rows = rows_of(away_own_tok, away_own_hidden)
    away_near_rows = rows_of(away_near_tok, away_near_hidden)
    by_group = doubled(weights, group_bits, "groups")[weights.shape[0] :]
    by_chip = hop(weights, low_bit)
    first = jnp.concatenate([weights, by_group, by_chip])
    lower, upper = by_group[:, :upper_row], by_chip[:, upper_row:]
    (
        far_in, own_hidden, away_far_tok, away_near_hidden, away_own_rows, away_near_rows,
        first, lower, upper,
    ) = settle_round(
        2, far_in, own_hidden, away_far_tok, away_near_hidden, away_own_rows, away_near_rows,
        first, lower, upper,
    )

    near_hidden = hop(away_near_hidden, half)
    away_others = hop(jnp.concatenate([away_own_rows[1], away_near_rows[1]]), 1)
    chip_count = upper.shape[0]
    lower = hop(lower, low_bit)
    upper = doubled(upper, group_bits, "groups")[chip_count:]
    first_other = hop(first, 1)
    far_in, own_hidden, away_others = settle(far_in, own_hidden, away_others)
    away_far_hidden = hidden_of(away_far_tok, far_in)
    away_far_rows = rows_of(away_far_tok, away_far_hidden)
    own_rows = rows_of(own_tok, own_hidden)
    (
        near_hidden, away_others, away_far_hidden, away_far_rows, own_rows, first, first_other,
        lower, upper,
    ) = settle(
        near_hidden, away_others, away_far_hidden, away_far_rows, own_rows, first, first_other,
        lower, upper,
    )

    far_hidden = hop(away_far_hidden, half)
    second = jnp.concatenate([lower, upper])
    stacks = first, second, first_other, hop(second, 1)
    shared_own, shared_other = shared_sums(stacks)
    near_hidden, shared_own = settle(near_hidden, shared_own)
    parts = hops_of(summed(away_near_rows[0], away_others[1:]), near_chips)
    others = hop(jnp.concatenate([own_rows[1], away_far_rows[1]]), 1)
    near_rows = rows_of(near_tok, near_hidden)
    far_hidden, stacks, shared_own, shared_other, parts, others, near_rows = settle(
        far_hidden, stacks, shared_own, shared_other, parts, others, near_rows
    )

    shared_in = hop(shared_own, half)
    parts += hops_of(summed(away_far_rows[0], others[1:]), far_chips)
    near_others = hop(near_rows[1], 1)
    far_rows = rows_of(far_tok, far_hidden)
    shared_in, parts, near_others, far_rows = settle(shared_in, parts, near_others, far_rows)

    total = shared_other + shared_in.astype(f32)
    other_hidden = (silu(total[:, :units]) * total[:, units:]).astype(bf16)
    shared_hidden = hop(other_hidden, half)
    shared_out = shared_down_of(other_hidden, stacks)
    away_rows = finished(shared_out, away_own_rows[0], away_others[0], parts)
    parts = hops_of(summed(near_rows[0], near_others), near_chips)
    far_others = hop(far_rows[1], 1)
    far_half = hop(away_rows, half)
    shared_hidden, parts[-1] = settle(shared_hidden, parts[-1])
    parts += hops_of(summed(far_rows[0], far_others), far_chips)
    shared_out = shared_down_of(shared_hidden, stacks)
    near_half = finished(shared_out, own_rows[0], others[0], parts)
    return ordered(is_upper, near_half, far_half, 1)


def solution(mesh):
    in_specs = (
        P(("groups", "expert"), None),
        P("expert", None),
        P(None, "expert"),
        P("expert", None),
        P(None, "expert"),
        P(),
        P(("groups", "expert"), None),
        P(("groups", "expert"), None),
    )
    out_specs = P(("groups", "expert"), None)
    return jax.shard_map(local, mesh=mesh, in_specs=in_specs, out_specs=out_specs, check_vma=False)
```

```python
import functools

import jax
import jax.numpy as jnp
from jax import lax
from jax.experimental import pallas as pl
from jax.experimental.pallas import tpu as pltpu
from jax.sharding import PartitionSpec as P

route_scale = 2.5
meta_lanes = 128
vmem_bytes = 48 * 1024 * 1024
f32 = jnp.float32
bf16 = jnp.bfloat16


def hop(block, mask, axis="expert"):
    count = lax.axis_size(axis)
    return lax.ppermute(block, axis, [(d, d ^ mask) for d in range(count)])


def settle_round(late, *values):
    last, rest = values[:late], lax.optimization_barrier(values[late:])
    last, rest = lax.optimization_barrier((last, rest))
    return last + rest


def settle(*values):
    return lax.optimization_barrier(values)


def ordered(is_upper, own_part, other_part, axis_dim):
    return jnp.where(
        is_upper,
        jnp.concatenate([other_part, own_part], axis_dim),
        jnp.concatenate([own_part, other_part], axis_dim),
    )


def silu(v):
    return v / (1.0 + jnp.exp(-v))


def slots_of(meta, pair, lanes):
    m = meta.astype(f32)
    rows = m.shape[0]
    first = m[:, 0:1] == pair
    second = m[:, 1:2] == pair
    gate = jnp.where(first, m[:, 2:3] + m[:, 3:4], 0.0) + jnp.where(
        second, m[:, 4:5] + m[:, 5:6], 0.0
    )
    hit = jnp.where(first, 1.0, 0.0) + jnp.where(second, 1.0, 0.0)
    before = lax.broadcasted_iota(jnp.int32, (rows, rows), 1) < lax.broadcasted_iota(
        jnp.int32, (rows, rows), 0
    )
    wide_hit = jnp.broadcast_to(hit, (rows, lanes))
    rank = jnp.dot(
        jnp.where(before, 1.0, 0.0).astype(bf16), wide_hit.astype(bf16), preferred_element_type=f32
    )
    slot = lax.broadcasted_iota(jnp.int32, (rows, lanes), 1).astype(f32)
    one_hot = jnp.where(rank == slot, wide_hit, 0.0).astype(bf16)
    return one_hot, gate


def pick_rows(pair_ref, first_ref, second_ref, rows_ref, cap):
    width = rows_ref.shape[1]
    count = first_ref.shape[1]
    pair = pair_ref[0].astype(f32)
    lanes = -(-cap // 128) * 128
    dims = (((0,), (0,)), ((), ()))
    for q in range(first_ref.shape[0]):
        meta = jnp.concatenate([first_ref[q, :, width:], second_ref[q, :, width:]], 0)
        one_hot, _ = slots_of(meta, pair, lanes)
        rows = lax.dot_general(
            one_hot[:count], first_ref[q, :, :width], dims, preferred_element_type=f32
        ) + lax.dot_general(
            one_hot[count:], second_ref[q, :, :width], dims, preferred_element_type=f32
        )
        rows_ref[q * cap : (q + 1) * cap, :] = rows[:cap].astype(bf16)


def partial_kernel(cap, pair_ref, first_ref, second_ref, w_ref, out_ref, rows_ref):
    @pl.when(pl.program_id(0) == 0)
    def _():
        pick_rows(pair_ref, first_ref, second_ref, rows_ref, cap)

    out_ref[...] = jnp.dot(
        rows_ref[...], w_ref[...], preferred_element_type=f32
    ).astype(bf16)


def hidden_kernel(
    cap, pair_ref, first_ref, second_ref, wg_ref, wu_ref, rg_ref, ru_ref, out_ref, rows_ref
):
    @pl.when(pl.program_id(0) == 0)
    def _():
        pick_rows(pair_ref, first_ref, second_ref, rows_ref, cap)

    rows = rows_ref[...]
    gate = jnp.dot(rows, wg_ref[...], preferred_element_type=f32) + rg_ref[...].astype(f32)
    up = jnp.dot(rows, wu_ref[...], preferred_element_type=f32) + ru_ref[...].astype(f32)
    out_ref[...] = (silu(gate) * up).astype(bf16)


def down_kernel(
    cap,
    pair_ref,
    first_ref,
    second_ref,
    hid_ref,
    w_ref,
    near_ref,
    far_ref,
    hit_ref,
    gate_ref,
    rows_ref,
):
    chips, count, _ = near_ref.shape

    @pl.when(pl.program_id(0) == 0)
    def _():
        for q in range(chips):
            meta = jnp.concatenate([first_ref[q], second_ref[q]], 0)
            one_hot, gate = slots_of(meta, pair_ref[0].astype(f32), hit_ref.shape[2])
            hit_ref[q] = one_hot
            gate_ref[q] = jnp.broadcast_to(gate, gate_ref.shape[1:])
        rows_ref[...] = jnp.zeros_like(rows_ref)

    rows = jnp.dot(hid_ref[...], w_ref[...], preferred_element_type=f32).astype(bf16)
    for q in range(chips):
        rows_ref[q, :cap, :] = rows[q * cap : (q + 1) * cap]
        picked = jnp.dot(hit_ref[q], rows_ref[q], preferred_element_type=f32)
        gated = (picked * gate_ref[q, :, 0:1]).astype(bf16)
        near_ref[q] = gated[:count]
        far_ref[q] = gated[count:]


def params():
    return pltpu.CompilerParams(
        vmem_limit_bytes=vmem_bytes, dimension_semantics=("arbitrary",)
    )


def smem():
    return pl.BlockSpec(memory_space=pltpu.SMEM)


def whole(array):
    return pl.BlockSpec(array.shape, lambda j: (0,) * len(array.shape))


def cost(m, k, n):
    return pl.CostEstimate(flops=0, bytes_accessed=0, transcendentals=0)


def partial_sums(pair, tok, weights, cap):
    width, columns = weights.shape
    rows = tok[0].shape[0] * cap
    steps = 4
    return pl.pallas_call(
        functools.partial(partial_kernel, cap),
        grid=(steps,),
        in_specs=[
            smem(),
            whole(tok[0]),
            whole(tok[1]),
            pl.BlockSpec((width, columns // steps), lambda j: (0, j)),
        ],
        out_specs=pl.BlockSpec((rows, columns // steps), lambda j: (0, j)),
        out_shape=jax.ShapeDtypeStruct((rows, columns), bf16),
        scratch_shapes=[pltpu.VMEM((rows, width), bf16)],
        compiler_params=params(),
        cost_estimate=cost(rows, width, columns),
    )(pair, *tok, weights)


def hidden_rows(pair, tok, weights, received, cap):
    width, columns = weights.shape
    units = columns // 2
    rows = received.shape[0]
    steps = 4
    block = units // steps
    return pl.pallas_call(
        functools.partial(hidden_kernel, cap),
        grid=(steps,),
        in_specs=[
            smem(),
            whole(tok[0]),
            whole(tok[1]),
            pl.BlockSpec((width, block), lambda j: (0, j)),
            pl.BlockSpec((width, block), lambda j: (0, j + steps)),
            pl.BlockSpec((rows, block), lambda j: (0, j)),
            pl.BlockSpec((rows, block), lambda j: (0, j + steps)),
        ],
        out_specs=pl.BlockSpec((rows, block), lambda j: (0, j)),
        out_shape=jax.ShapeDtypeStruct((rows, units), bf16),
        scratch_shapes=[pltpu.VMEM((rows, width), bf16)],
        compiler_params=params(),
        cost_estimate=cost(rows, width, columns),
    )(pair, *tok, weights, weights, received, received)


def weighted_rows(pair, tok, hidden, weights, cap):
    units, width = weights.shape
    chips, count, _ = tok[0].shape
    lanes = -(-cap // 128) * 128
    steps = 2
    block = width // steps
    meta = pl.BlockSpec((chips, count, meta_lanes), lambda j: (0, 0, width // meta_lanes))
    return pl.pallas_call(
        functools.partial(down_kernel, cap),
        grid=(steps,),
        in_specs=[
            smem(),
            meta,
            meta,
            whole(hidden),
            pl.BlockSpec((units, block), lambda j: (0, j)),
        ],
        out_specs=[pl.BlockSpec((chips, count, block), lambda j: (0, 0, j))] * 2,
        out_shape=[jax.ShapeDtypeStruct((chips, count, width), bf16)] * 2,
        scratch_shapes=[
            pltpu.VMEM((chips, 2 * count, lanes), bf16),
            pltpu.VMEM((chips, 2 * count, 128), f32),
            pltpu.VMEM((chips, lanes, block), bf16),
        ],
        compiler_params=params(),
        cost_estimate=cost(chips * cap, units, width),
    )(pair, *tok, hidden, weights)


def assemble(masks, first_column, spots_ref, stack_refs, out_ref, sems):
    count = len(masks)
    columns = out_ref.shape[1] // len({q for _, _, q in masks})
    shard_rows = out_ref.shape[0] // len({m for _, m, _ in masks}) // 2
    places = [(ref, i) for ref in stack_refs for i in range(ref.shape[0])]
    copies = []
    for at, (stack_ref, i) in enumerate(places):
        upper, _, q = masks[at % count]
        rows = stack_ref.shape[1]
        row = pl.multiple_of(spots_ref[at] * shard_rows + upper * rows, rows)
        column = pl.multiple_of(spots_ref[2 * count + q] * columns, columns)
        copies.append(
            pltpu.make_async_copy(
                stack_ref.at[i, :, pl.ds(first_column, columns)],
                out_ref.at[pl.ds(row, rows), pl.ds(column, columns)],
                sems.at[at],
            )
        )
    for copy in copies:
        copy.start()
    for copy in copies:
        copy.wait()


def shared_gate_kernel(masks, spots_ref, own_ref, other_ref, *refs):
    stack_refs, (mine_ref, theirs_ref, w_ref, sems) = refs[:-4], refs[-4:]
    assemble(masks, 0, spots_ref, stack_refs, w_ref, sems)
    width, columns = w_ref.shape
    step = 512

    @pl.loop(0, columns // step)
    def _(j):
        at = pl.ds(pl.multiple_of(j * step, step), step)
        w = w_ref[:, at]
        mine_ref[:, at] = jnp.dot(own_ref[:, :width], w, preferred_element_type=f32).astype(bf16)
        theirs_ref[:, at] = jnp.dot(other_ref[:, :width], w, preferred_element_type=f32)


def shared_partial(spots, masks, own, other, stacks, width, columns):
    rows = own.shape[0]
    vmem = pl.BlockSpec(memory_space=pltpu.VMEM)
    hbm = pl.BlockSpec(memory_space=pl.ANY)
    return pl.pallas_call(
        functools.partial(shared_gate_kernel, masks),
        in_specs=[smem(), vmem, vmem] + [hbm] * len(stacks),
        out_specs=[vmem, vmem],
        out_shape=[
            jax.ShapeDtypeStruct((rows, columns), bf16),
            jax.ShapeDtypeStruct((rows, columns), f32),
        ],
        scratch_shapes=[
            pltpu.VMEM((width, columns), bf16),
            pltpu.SemaphoreType.DMA((2 * len(masks),)),
        ],
        compiler_params=pltpu.CompilerParams(vmem_limit_bytes=vmem_bytes),
        cost_estimate=cost(2 * rows, width, columns),
    )(spots, own, other, *stacks)


def shared_down_kernel(masks, first_column, spots_ref, hid_ref, *refs):
    stack_refs, (out_ref, d_ref, sems) = refs[:-3], refs[-3:]
    assemble(masks, first_column, spots_ref, stack_refs, d_ref, sems)
    step = 256

    @pl.loop(0, d_ref.shape[0] // step)
    def _(j):
        at = pl.ds(pl.multiple_of(j * step, step), step)
        out_ref[:, at] = lax.dot_general(
            hid_ref[...], d_ref[at, :], (((1,), (1,)), ((), ())), preferred_element_type=f32
        ).astype(bf16)


def shared_rows(spots, masks, hidden, stacks, first_column, width):
    rows, units = hidden.shape
    vmem = pl.BlockSpec(memory_space=pltpu.VMEM)
    hbm = pl.BlockSpec(memory_space=pl.ANY)
    return pl.pallas_call(
        functools.partial(shared_down_kernel, masks, first_column),
        in_specs=[smem(), vmem] + [hbm] * len(stacks),
        out_specs=vmem,
        out_shape=jax.ShapeDtypeStruct((rows, width), bf16),
        scratch_shapes=[
            pltpu.VMEM((width, units), bf16),
            pltpu.SemaphoreType.DMA((2 * len(masks),)),
        ],
        compiler_params=pltpu.CompilerParams(vmem_limit_bytes=vmem_bytes),
        cost_estimate=cost(rows, units, width),
    )(spots, hidden, *stacks)


def in_order(masks, place, group_index, stacks):
    groups = len({q for _, _, q in masks})
    shards = 2 * len({m for _, m, _ in masks})
    rows = min(stack.shape[1] for stack in stacks)
    pieces = [
        (stack[i : i + 1, at : at + rows], i_mask, stack.shape[1] > rows and at > 0)
        for stack, i, i_mask in numbered(masks, stacks)
        for at in range(0, stack.shape[1], rows)
    ]
    spot = {}
    for number, (_, (core, upper, m, q), second) in enumerate(pieces):
        spot[m | core, 1 if second else upper, q] = number
    table = [[[spot[m, u, q] for q in range(groups)] for u in (0, 1)] for m in range(shards)]
    table = jnp.array(table, jnp.int32)
    table = table[jnp.arange(shards, dtype=jnp.int32) ^ place]
    table = table[:, :, jnp.arange(groups, dtype=jnp.int32) ^ group_index]
    parts = jnp.concatenate([piece for piece, _, _ in pieces])[table]
    parts = parts.transpose(0, 1, 3, 2, 4)
    return parts.reshape(shards, -1, groups, parts.shape[-1])


def numbered(masks, stacks):
    places = [(stack, i) for stack in stacks for i in range(stack.shape[0])]
    count = len(masks)
    return [
        (stack, i, (at // count,) + masks[at % count]) for at, (stack, i) in enumerate(places)
    ]


def local(
    tokens,
    expert_gate_up,
    expert_down,
    shared_gate_up,
    shared_down,
    host_expert,
    pair_picks,
    affinity,
):
    devices = lax.axis_size("expert")
    groups = lax.axis_size("groups")
    half = devices // 2
    dev_index = lax.axis_index("expert")
    group_index = lax.axis_index("groups")
    is_upper = dev_index >= half
    pair = jnp.reshape(dev_index % half, (1,)).astype(jnp.int32)
    tok_rows, full_width = tokens.shape
    width = full_width // 2
    units = expert_down.shape[0]
    pick_count = pair_picks.shape[1]
    capacity = 7 * tok_rows * pick_count // (4 * half)
    cap = -(-2 * capacity // 16) * 16
    chips = list(range(2, half, 2))
    near_chips = sorted([m for m in chips if m & (m - 1) == 0], reverse=True)
    far_chips = [m for m in chips if m & (m - 1)]

    pair_iota = jnp.arange(half, dtype=jnp.int32)
    expert_ids = jnp.sum(
        jnp.where(pair_picks[:, :, None] == pair_iota, host_expert[None, None, :], 0), 2
    )
    scores = jnp.sum(
        jnp.where(expert_ids[:, :, None] == pair_iota, affinity[:, None, :], 0.0), 2
    )
    gates = route_scale * scores / jnp.sum(scores, 1, keepdims=True)
    gates_high = lax.reduce_precision(gates, 8, 7)
    gates_low = gates - gates_high
    meta = jnp.concatenate(
        [
            pair_picks.astype(f32),
            jnp.stack([gates_high, gates_low], 2).reshape(tok_rows, 2 * pick_count),
            jnp.zeros((tok_rows, meta_lanes - 3 * pick_count), f32),
        ],
        1,
    ).astype(bf16)
    low, high = tokens[:, :width], tokens[:, width:]
    mine = jnp.concatenate([jnp.where(is_upper, high, low), meta], 1)
    theirs = jnp.concatenate([jnp.where(is_upper, low, high), meta], 1)

    def sums_of(tok):
        return partial_sums(pair, tok, expert_gate_up, cap)

    def hidden_of(tok, sums):
        return hidden_rows(pair, tok, expert_gate_up, sums, cap)

    def rows_of(tok, hidden):
        return weighted_rows(pair, tok, hidden, expert_down, cap)

    def summed(rows, other):
        return (rows.astype(f32) + other.astype(f32)).astype(bf16)

    def hops_of(blocks, masks):
        return [hop(block, m) for m, block in zip(masks, blocks)]

    def finished(shared, rows, other, parts):
        total = shared.astype(f32) + rows[0].astype(f32) + other.astype(f32)
        for part in parts:
            total = total + part.astype(f32)
        return total.astype(bf16)

    low_bit, later_bits = near_chips[-1], near_chips[:-1]
    group_bits = [1 << i for i in range(groups.bit_length() - 1)]
    gate_columns = 2 * units // groups
    down_rows = units // groups
    shard_rows = shared_gate_up.shape[0]
    upper_row = shard_rows // 2

    def share_of_weights():
        gate = lax.dynamic_slice_in_dim(shared_gate_up, group_index * gate_columns, gate_columns, 1)
        down = lax.dynamic_slice_in_dim(shared_down, group_index * down_rows, down_rows, 0)
        return jnp.concatenate([gate, down.T], 1)[None]

    def doubled(stack, bits, axis="expert"):
        for bit in bits:
            stack = jnp.concatenate([stack, hop(stack, bit, axis)])
        return stack

    def masks_of(upper, steps):
        masks = [(0, 0)]
        for m, q in steps:
            masks = masks + [(a ^ m, b ^ q) for a, b in masks]
        return [(upper, a, b) for a, b in masks]

    start_masks = masks_of(0, [(m, 0) for m in later_bits])
    all_groups = masks_of(0, [(m, 0) for m in later_bits] + [(0, q) for q in group_bits])
    other_groups = all_groups[len(start_masks) :]
    masks = start_masks + other_groups + [(0, m ^ low_bit, q) for _, m, q in start_masks]
    masks += [(upper, m ^ low_bit, q) for upper in (0, 1) for _, m, q in other_groups]
    place = dev_index % half
    chip_masks = jnp.array([m for _, m, _ in masks], jnp.int32)
    spots = jnp.concatenate(
        [place ^ chip_masks, place ^ 1 ^ chip_masks, group_index ^ jnp.arange(groups)]
    ).astype(jnp.int32)
    by_kernel = upper_row % 16 == 0

    def shared_sums(stacks):
        if by_kernel:
            return shared_partial(spots, masks, mine, cross, stacks, width, 2 * units)
        gate = in_order(masks, place, group_index, stacks)[..., :gate_columns]
        gate = gate.reshape(width, 2 * units)
        own = jnp.dot(mine[:, :width], gate, preferred_element_type=f32).astype(bf16)
        return own, jnp.dot(cross[:, :width], gate, preferred_element_type=f32)

    def shared_down_of(hidden, stacks):
        if by_kernel:
            return shared_rows(spots, masks, hidden, stacks, gate_columns, width)
        down = in_order(masks, place, group_index, stacks)[..., gate_columns:]
        down = down.reshape(width, units)
        return lax.dot_general(
            hidden, down, (((1,), (1,)), ((), ())), preferred_element_type=f32
        ).astype(bf16)

    cross = hop(theirs, half)
    near = [hop(mine, m) for m in near_chips]
    own_tok = mine[None], hop(mine, 1)[None]
    own_sums = sums_of(own_tok)
    weights = share_of_weights()
    cross, near, own_tok, own_sums, weights = settle(cross, near, own_tok, own_sums, weights)

    own_in = hop(own_sums, half)
    got = dict(zip(near_chips, near))
    away_near = [hop(cross, m) for m in near_chips[:-1]]
    near_tok = jnp.stack(near)
    near_tok = near_tok, hop(near_tok, 1)
    first_far = [m for m in far_chips if m & low_bit]
    later_far = [m for m in far_chips if not m & low_bit]
    for m in sorted(later_far):
        got[m] = hop(got[m ^ (m & -m)], m & -m)
    both = hop(jnp.stack([cross] + [got[m ^ low_bit] for m in first_far]), low_bit)
    away_near.append(both[0])
    for i, m in enumerate(first_far):
        got[m] = both[1 + i]
    far = [got[m] for m in far_chips]
    near_sums = sums_of(near_tok)
    own_in, away_near, far, near_tok, near_sums = settle(
        own_in, away_near, far, near_tok, near_sums
    )

    near_in = hop(near_sums, half)
    got = dict(zip(near_chips, away_near))
    for m in sorted(far_chips, key=lambda m: bin(m).count("1")):
        got[m] = hop(got[m ^ (m & -m)], m & -m)
    away_far = [got[m] for m in far_chips]
    mixed = jnp.stack([cross] + away_near + far)
    others = hop(mixed, 1)
    cut = 1 + len(near_chips)
    away_own_tok = mixed[:1], others[:1]
    away_near_tok = mixed[1:cut], others[1:cut]
    far_tok = mixed[cut:], others[cut:]
    far_sums = sums_of(far_tok)
    away_own_hidden = hidden_of(away_own_tok, own_in)
    weights = doubled(weights, later_bits)
    (
        near_in, away_far, away_near_tok, away_own_tok, far_tok, far_sums, away_own_hidden, weights
    ) = settle(
        near_in, away_far, away_near_tok, away_own_tok, far_tok, far_sums, away_own_hidden, weights
    )

    far_in = hop(far_sums, half)
    own_hidden = hop(away_own_hidden, half)
    away_far_tok = jnp.stack(away_far)
    away_far_tok = away_far_tok, hop(away_far_tok, 1)
    away_near_hidden = hidden_of(away_near_tok, near_in)
    away_own_rows = rows_of(away_own_tok, away_own_hidden)
    away_near_rows = rows_of(away_near_tok, away_near_hidden)
    by_group = doubled(weights, group_bits, "groups")[weights.shape[0] :]
    by_chip = hop(weights, low_bit)
    first = jnp.concatenate([weights, by_group, by_chip])
    lower, upper = by_group[:, :upper_row], by_chip[:, upper_row:]
    (
        far_in, own_hidden, away_far_tok, away_near_hidden, away_own_rows, away_near_rows,
        first, lower, upper,
    ) = settle_round(
        2, far_in, own_hidden, away_far_tok, away_near_hidden, away_own_rows, away_near_rows,
        first, lower, upper,
    )

    near_hidden = hop(away_near_hidden, half)
    away_others = hop(jnp.concatenate([away_own_rows[1], away_near_rows[1]]), 1)
    chip_count = upper.shape[0]
    lower = hop(lower, low_bit)
    upper = doubled(upper, group_bits, "groups")[chip_count:]
    first_other = hop(first, 1)
    far_in, own_hidden, away_others = settle(far_in, own_hidden, away_others)
    away_far_hidden = hidden_of(away_far_tok, far_in)
    away_far_rows = rows_of(away_far_tok, away_far_hidden)
    own_rows = rows_of(own_tok, own_hidden)
    blocks = list(summed(away_near_rows[0], away_others[1:]))
    others = jnp.concatenate([own_rows[1], away_far_rows[1]])
    (
        near_hidden, blocks, others, away_others, away_far_hidden, away_far_rows, own_rows, first,
        first_other, lower, upper,
    ) = settle_round(
        1, near_hidden, blocks, others, away_others, away_far_hidden, away_far_rows, own_rows,
        first, first_other, lower, upper,
    )

    far_hidden = hop(away_far_hidden, half)
    second = jnp.concatenate([lower, upper])
    stacks = first, second, first_other, hop(second, 1)
    shared_own, shared_other = shared_sums(stacks)
    near_hidden, shared_own = settle(near_hidden, shared_own)
    parts = hops_of(blocks, near_chips)
    others = hop(others, 1)
    near_rows = rows_of(near_tok, near_hidden)
    blocks = list(summed(away_far_rows[0], others[1:]))
    far_hidden, parts, stacks, shared_own, shared_other, others, near_rows, blocks = settle_round(
        2, far_hidden, parts, stacks, shared_own, shared_other, others, near_rows, blocks
    )

    shared_in = hop(shared_own, half)
    parts += hops_of(blocks, far_chips)
    near_others = hop(near_rows[1], 1)
    far_rows = rows_of(far_tok, far_hidden)
    shared_in, parts, near_others, far_rows = settle(shared_in, parts, near_others, far_rows)

    total = shared_other + shared_in.astype(f32)
    other_hidden = (silu(total[:, :units]) * total[:, units:]).astype(bf16)
    shared_hidden = hop(other_hidden, half)
    shared_out = shared_down_of(other_hidden, stacks)
    away_rows = finished(shared_out, away_own_rows[0], away_others[0], parts)
    parts = hops_of(summed(near_rows[0], near_others), near_chips)
    far_others = hop(far_rows[1], 1)
    far_half = hop(away_rows, half)
    shared_hidden, parts[-1] = settle(shared_hidden, parts[-1])
    parts += hops_of(summed(far_rows[0], far_others), far_chips)
    shared_out = shared_down_of(shared_hidden, stacks)
    near_half = finished(shared_out, own_rows[0], others[0], parts)
    return ordered(is_upper, near_half, far_half, 1)


def solution(mesh):
    in_specs = (
        P(("groups", "expert"), None),
        P("expert", None),
        P(None, "expert"),
        P("expert", None),
        P(None, "expert"),
        P(),
        P(("groups", "expert"), None),
        P(("groups", "expert"), None),
    )
    out_specs = P(("groups", "expert"), None)
    return jax.shard_map(local, mesh=mesh, in_specs=in_specs, out_specs=out_specs, check_vma=False)
```
